32 devices in a mesh: runs: 2 (over y), gx: 4 (over z), gy: 2 (over x), gz: 2 (over core).
Axes of the slice: x: 2, y: 2, z: 4, core: 2. Of those that a mesh axis runs over, the one named last changes fastest.
Arguments:
- row_owner: int32 [16384], P(('runs', 'gx', 'gy', 'gz')), parts along dimension 0, may hold values from 0 to 15, as said below
- row_count: int32 [16384], P(('runs', 'gx', 'gy', 'gz')), parts along dimension 0, may hold values from 1 to 128
- row_block: int32 [16384], P(('runs', 'gx', 'gy', 'gz')), parts along dimension 0, may hold values from 0 to 8191
- offsets: float32 [3, 16384, 128], P(None, ('runs', 'gx', 'gy', 'gz')), parts along dimension 1, may hold values from 0 to 2
- particle_mass: float32 [16384, 128], P(('runs', 'gx', 'gy', 'gz')), parts along dimension 0, may hold values from 0.25 to 4
- particle_velocity: float32 [3, 16384, 128], P(None, ('runs', 'gx', 'gy', 'gz')), parts along dimension 1, may hold values from -18 to 18
- material: int32 [64, 128, 256], P(('runs', 'gx'), 'gy', 'gz'), parts along dimension 0, may hold values from 0 to 7
- stiffness: float32 [8], replicated, may hold values from 0.02 to 0.16
Outputs:
- node_mass: float32 [64, 128, 256], P(('runs', 'gx'), 'gy', 'gz'), parts along dimension 0
- node_velocity: float32 [3, 64, 128, 256], P(None, ('runs', 'gx'), 'gy', 'gz'), parts along dimension 1
The draws below stay inside these ranges and needn't reach their ends.
There are 2 independent parts, one for each index of `runs`. The reference program is written for one: setup_inputs(seed, part) draws one part's arguments, and reference() takes and returns one part's arrays. A program takes and returns all parts, laid end to end along the dimension named above; an argument that names none is the same for every part. Nothing has to cross between parts.
Inputs may be any that keep to these rules, and one draw needn't show every extreme that they name: row_owner is the index over gx, gy, gz together (gx slowest) of the row's holder or of a device next to it along exactly one of the three axes; no holder gives more than 4 rows to one other device, and in every draw some holder gives exactly 4 rows to one neighbour.
All inputs are finite; a program needn't handle non-finite values.
Results may differ from the reference program's by a relative error of at most 0.0003.
Values sent between devices are 32-bit elements; how exact they have to be, the bound alone decides.
A program may use at most 64 MiB of HBM per device.

```python
import math
import jax
import jax.numpy as jnp
from jax import lax

CX = 8
CY = 64
CZ = 128
ROWS_DEV = 512
CAP = 4
SLOTS = 128
MATS = 8
NB = 8192
NX = 32
NY = 128
NZ = 256
ROWS = 8192
N_GX = 4
N_GY = 2
N_GZ = 2


def draw_row_owner(key, part):
    key = jax.random.fold_in(key, 11)
    first_key, second_key = jax.random.split(key)
    group_size = N_GX * N_GY * N_GZ
    devices = jnp.arange(group_size).astype(jnp.int32)
    coord_x = devices // (N_GY * N_GZ)
    coord_y = devices // N_GZ % N_GY
    coord_z = devices % N_GZ
    allowed = jnp.stack([coord_x > 0, coord_x < N_GX - 1, coord_y > 0, coord_y < N_GY - 1, coord_z > 0, coord_z < N_GZ - 1], 1)
    leaving = jax.random.randint(first_key, (group_size, 6), 0, CAP + 1).astype(jnp.int32)
    leaving = jnp.where(allowed, leaving, 0)
    leaving = leaving.at[0, 1].set(CAP)
    bounds = jnp.cumsum(leaving, 1)
    orders = jax.vmap(lambda single: jax.random.permutation(single, ROWS_DEV))(jax.random.split(second_key, group_size)).astype(jnp.int32)
    places = jnp.zeros((group_size, ROWS_DEV), jnp.int32).at[devices[:, None], orders].set(jnp.arange(ROWS_DEV).astype(jnp.int32)[None, :])
    direction = jnp.sum((places[:, :, None] >= bounds[:, None, :]).astype(jnp.int32), 2)
    steps_table = jnp.array([-N_GY * N_GZ, N_GY * N_GZ, -N_GZ, N_GZ, -1, 1, 0], jnp.int32)
    owners = devices[:, None] + steps_table[direction]
    return owners.reshape(-1).astype(jnp.int32)


def plant(result, rng, smallest, high):
    longest = result.shape.index(max(result.shape))
    spots = []
    for shift in (0, 1):
        where = [jax.random.randint(jax.random.fold_in(rng, axis), (), 0, length) for axis, length in enumerate(result.shape)]
        where[longest] = (where[longest] + shift) % result.shape[longest]
        spots.append(tuple(where))
    return result.at[spots[0]].set(smallest).at[spots[1]].set(high)


def steps_of(stream_key, shape, cuts, least, top_value):
    def one(position, shards_of):
        heights = jax.random.uniform(jax.random.fold_in(jax.random.fold_in(stream_key, 6), position), (shards_of,), jnp.float32, least / len(cuts), top_value / len(cuts))
        return jnp.repeat(jnp.exp(heights), shape[position] // shards_of).reshape((-1,) + (1,) * (len(shape) - position - 1))

    gain = one(*cuts[0])
    for cut in cuts[1:]:
        gain = gain * one(*cut)
    return gain


def gaussian(rng, extent, scale, reach, pieces=(), held_as=jnp.bfloat16):
    entries = jax.random.normal(rng, extent, jnp.float32) * scale
    if len(pieces) > 0:
        entries = steps_of(rng, extent, pieces, -0.22, 0.18) * entries
    return jnp.clip(entries, min=-reach, max=reach).astype(held_as)


def setup_inputs(seed: int = 0, part: int = 0) -> dict:
    seeds = jax.random.split(jax.random.key(seed), 9)
    part_splits = jax.random.split(jax.random.fold_in(seeds[8], part), 9)
    return {
        "row_owner": draw_row_owner(jax.random.fold_in(jax.random.fold_in(seeds[8], part), 71), part),
        "row_count": plant(jax.random.randint(part_splits[1], (ROWS,), 1, SLOTS + 1), jax.random.fold_in(part_splits[1], 1), 1, SLOTS).astype(jnp.int32),
        "row_block": plant(jax.random.randint(part_splits[2], (ROWS,), 0, NB), jax.random.fold_in(part_splits[2], 1), 0, NB - 1).astype(jnp.int32),
        "offsets": jnp.clip(2.0 * jax.random.uniform(part_splits[3], (3, ROWS, SLOTS), jnp.float32) ** steps_of(part_splits[3], (3, ROWS, SLOTS), ((1, 16),), -0.2, 0.2), 0.0, 2.0),
        "particle_mass": jnp.clip(jnp.exp(math.log(4.0) - 2.7725887 * jax.random.uniform(part_splits[4], (ROWS, SLOTS), jnp.float32) ** steps_of(part_splits[4], (ROWS, SLOTS), ((0, 16),), -0.2, 0.2)), 0.25, 4.0),
        "particle_velocity": gaussian(part_splits[5], (3, ROWS, SLOTS), 3.0, 18.0, ((1, 16),), jnp.float32),
        "material": plant(jax.random.randint(part_splits[6], (NX, NY, NZ), 0, MATS), jax.random.fold_in(part_splits[6], 1), 0, MATS - 1).astype(jnp.int32),
        "stiffness": jnp.clip(jnp.exp(jax.random.uniform(seeds[7], (MATS,), jnp.float32, math.log(0.02), math.log(0.16))), 0.02, 0.16),
    }


gravity_step = 0.05


def spline(positions):
    node_step = jnp.arange(4).astype(jnp.float32)[:, None]
    distance = jnp.abs(positions[..., None, :] + 0.5 - node_step)
    inside_part = 0.75 - distance * distance
    outer_part = 0.5 * (1.5 - distance) * (1.5 - distance)
    return jnp.where(distance < 0.5, inside_part, jnp.where(distance < 1.5, outer_part, 0.0))


def patches(positions, masses, speeds):
    row_total = masses.shape[0]
    slot_total = masses.shape[1]
    weight_x = spline(positions[0])
    weight_y = spline(positions[1])
    weight_z = spline(positions[2])
    carried = jnp.stack([masses, masses * speeds[0], masses * speeds[1], masses * speeds[2]], 1)
    left_part = (weight_x[:, :, None, :] * weight_y[:, None, :, :]).reshape(row_total, 16, slot_total)
    right_part = (carried[:, :, None, :] * weight_z[:, None, :, :]).reshape(row_total, 16, slot_total)
    stencil = jnp.einsum("nip,njp->nij", left_part, right_part, precision=lax.Precision.HIGHEST)
    return stencil.reshape(row_total, 4, 4, 4, 4)


def reference(row_owner, row_count, row_block, offsets, particle_mass, particle_velocity, material, stiffness):
    group_size = N_GX * N_GY * N_GZ
    ext_x = NX + 2
    ext_y = NY + 2
    ext_z = NZ + 2
    half_y = CY // 2
    half_z = CZ // 2
    slot_iota = jnp.arange(SLOTS).astype(jnp.int32)
    node_steps = jnp.arange(4).astype(jnp.int32)

    def deposit(device, grid_flat):
        row_start = (device * ROWS_DEV).astype(jnp.int32)
        owners = lax.dynamic_slice_in_dim(row_owner, row_start, ROWS_DEV, 0)
        counts = lax.dynamic_slice_in_dim(row_count, row_start, ROWS_DEV, 0)
        blocks = lax.dynamic_slice_in_dim(row_block, row_start, ROWS_DEV, 0)
        positions = lax.dynamic_slice_in_dim(offsets, row_start, ROWS_DEV, 1)
        masses = lax.dynamic_slice_in_dim(particle_mass, row_start, ROWS_DEV, 0)
        speeds = lax.dynamic_slice_in_dim(particle_velocity, row_start, ROWS_DEV, 1)
        live_slots = (slot_iota[None, :] < counts[:, None]).astype(jnp.float32)
        stencil = patches(positions, masses * live_slots, speeds)
        coord_x = owners // (N_GY * N_GZ)
        coord_y = (owners // N_GZ) % N_GY
        coord_z = owners % N_GZ
        base_x = coord_x * CX + 2 * (blocks // (half_y * half_z))
        base_y = coord_y * CY + 2 * ((blocks // half_z) % half_y)
        base_z = coord_z * CZ + 2 * (blocks % half_z)
        index_x = base_x[:, None, None, None, None] + node_steps[None, :, None, None, None]
        index_y = base_y[:, None, None, None, None] + node_steps[None, None, :, None, None]
        channel = node_steps[None, None, None, :, None]
        index_z = base_z[:, None, None, None, None] + node_steps[None, None, None, None, :]
        flat_index = ((channel * ext_x + index_x) * ext_y + index_y) * ext_z + index_z
        return grid_flat.at[flat_index.reshape(-1)].add(stencil.reshape(-1))

    grid_flat = lax.fori_loop(0, group_size, deposit, jnp.zeros((4 * ext_x * ext_y * ext_z,), jnp.float32))
    node_grid = grid_flat.reshape(4, ext_x, ext_y, ext_z)[:, 1:-1, 1:-1, 1:-1]
    node_mass = node_grid[0]
    velocity = node_grid[1:] / jnp.maximum(node_mass, 1.0)[None]
    padded = jnp.pad(velocity, ((0, 0), (1, 1), (1, 1), (1, 1)))
    beside = padded[:, 2:, 1:-1, 1:-1] + padded[:, :-2, 1:-1, 1:-1]
    beside = beside + padded[:, 1:-1, 2:, 1:-1] + padded[:, 1:-1, :-2, 1:-1]
    beside = beside + padded[:, 1:-1, 1:-1, 2:] + padded[:, 1:-1, 1:-1, :-2]
    laplace = beside - 6.0 * velocity
    node_stiff = stiffness[material]
    updated = velocity + node_stiff[None] * laplace
    vertical = updated[2] - gravity_step
    bottom = (jnp.arange(NZ) == 0)[None, None, :]
    vertical = jnp.where(bottom, jnp.maximum(vertical, 0.0), vertical)
    node_velocity = jnp.stack([updated[0], updated[1], vertical], 0)
    return (node_mass, node_velocity)
```

```python
import functools

import jax
import jax.numpy as jnp
from jax import lax
from jax.experimental import pallas as pl
from jax.experimental.pallas import tpu as pltpu
from jax.sharding import PartitionSpec as P

CAP = 4
LANES = 128
gravity_step = 0.05
AXES = ("gx", "gy", "gz")
VMEM_LIMIT = 48 * 1024 * 1024


def spline(distance):
    distance = jnp.abs(distance)
    inside_part = 0.75 - distance * distance
    rest = jnp.maximum(1.5 - distance, 0.0)
    return jnp.where(distance < 0.5, inside_part, 0.5 * rest * rest)


def neighbours(counts):
    found = []
    for axis in AXES:
        here = lax.axis_index(axis)
        low = here > 0
        high = here < counts[axis] - 1
        found.append((axis, here - 1, low, high))
        found.append((axis, here + 1, high, low))
    return found


def greet(sides):
    barrier = pltpu.get_barrier_semaphore()
    total = 0
    for axis, target, there, _ in sides:
        @pl.when(there)
        def _():
            pl.semaphore_signal(
                barrier, inc=1, device_id={axis: target}, device_id_type=pl.DeviceIdType.MESH
            )
        total = total + there.astype(jnp.int32)
    pl.semaphore_wait(barrier, total)


def remote(source, target_ref, send_sem, recv_sem, axis, target):
    return pltpu.make_async_remote_copy(
        src_ref=source,
        dst_ref=target_ref,
        send_sem=send_sem,
        recv_sem=recv_sem,
        device_id={axis: target},
        device_id_type=pl.DeviceIdType.MESH,
    )


def rows_kernel(
    counts, owner_ref, count_ref, block_ref, offs_ref, mass_ref, vel_ref, box_ref, out_box, send_sem, recv_sem
):
    rows = mass_ref.shape[0]
    size_y, size_z = counts["gy"], counts["gz"]
    myself = (lax.axis_index("gx") * size_y + lax.axis_index("gy")) * size_z + lax.axis_index("gz")
    sides = neighbours(counts)
    box_ref[...] = jnp.zeros_like(box_ref)
    heading = owner_ref[...] - myself
    shape = heading.shape
    place = lax.broadcasted_iota(jnp.int32, shape, 0) * LANES + lax.broadcasted_iota(jnp.int32, shape, 1)
    lane = lax.broadcasted_iota(jnp.int32, (1, LANES), 1)
    steps = (-size_y * size_z, size_y * size_z, -size_z, size_z, -1, 1)
    left = [jnp.where(heading == step, place, rows) for step in steps]
    for slot in range(CAP):
        for way in range(6):
            first = jnp.min(left[way])
            left[way] = jnp.where(left[way] == first, rows, left[way])
            valid = first < rows
            row = jnp.minimum(first, rows - 1)
            live = jnp.where(valid, count_ref[row], 0)
            for j in range(3):
                out_box[way, slot, pl.ds(j, 1), :] = offs_ref[j, pl.ds(row, 1), :]
                out_box[way, slot, pl.ds(4 + j, 1), :] = vel_ref[j, pl.ds(row, 1), :]
            out_box[way, slot, pl.ds(3, 1), :] = jnp.where(lane < live, mass_ref[pl.ds(row, 1), :], 0.0)
            block = jnp.where(valid, block_ref[row], 0).astype(jnp.float32)
            out_box[way, slot, pl.ds(7, 1), :] = jnp.full((1, LANES), block, jnp.float32)
    greet(sides)
    copies = [
        remote(out_box.at[way], box_ref.at[way], send_sem.at[way], recv_sem.at[way], axis, target)
        for way, (axis, target, _, _) in enumerate(sides)
    ]
    for way, (_, _, there, _) in enumerate(sides):
        pl.when(there)(copies[way].start)
    for way, (_, _, there, other) in enumerate(sides):
        pl.when(there)(copies[way].wait_send)
        pl.when(other)(copies[way].wait_recv)


def deposit_kernel(
    half_y, half_z, planes, me_ref, owner_ref, count_ref, block_ref, came_ref,
    offs_ref, mass_ref, vel_ref, box_ref, out_ref, grid_ref, wx_ref, yk_ref, wz_ref,
):
    rows = mass_ref.shape[0]
    came = box_ref.shape[0]
    sub = lax.broadcasted_iota(jnp.int32, (8, LANES), 0)
    lane = lax.broadcasted_iota(jnp.int32, (8, LANES), 1)
    myself = me_ref[0]
    zero8 = jnp.zeros((8, LANES), jnp.float32)

    def clear(i, carry):
        grid_ref[i] = jnp.zeros(grid_ref.shape[1:], jnp.float32)
        return carry

    lax.fori_loop(0, grid_ref.shape[0], clear, 0)

    def fill(base, ox, oy, oz, carried):
        for a in range(4):
            wx_ref[pl.ds(base * 4 + a, 8, stride=4), :] = spline(ox + (0.5 - a))
            wy = spline(oy + (0.5 - a))
            for k in range(4):
                yk_ref[pl.ds(base * 16 + a * 4 + k, 8, stride=16), :] = wy * carried[k]
            wz_ref[pl.ds(base * 8 + a, 8, stride=8), :] = spline(oz + (0.5 - a))
            wz_ref[pl.ds(base * 8 + 4 + a, 8, stride=8), :] = zero8

    def prepare(i, carry):
        base = pl.multiple_of(i * 8, 8)
        live = jnp.zeros((8, LANES), jnp.int32)
        for s in range(8):
            count = jnp.where(owner_ref[base + s] == myself, count_ref[base + s], 0)
            live = jnp.where(sub == s, count, live)
        at = pl.ds(base, 8)
        mass = jnp.where(lane < live, mass_ref[at, :], 0.0)
        carried = [mass] + [mass * vel_ref[j, at, :] for j in range(3)]
        fill(base, offs_ref[0, at, :], offs_ref[1, at, :], offs_ref[2, at, :], carried)
        return carry

    lax.fori_loop(0, rows // 8, prepare, 0)
    for group in range(came // 64):
        part = [box_ref[pl.ds(group * 64 + c, 8, stride=8), :] for c in range(8)]
        carried = [part[3]] + [part[3] * part[4 + j] for j in range(3)]
        fill(rows + group * 8, part[0], part[1], part[2], carried)

    def stencil(row):
        parts = []
        yk = yk_ref[pl.ds(pl.multiple_of(row * 16, 16), 16), :]
        for a in range(4):
            parts.append(yk * wx_ref[pl.ds(row * 4 + a, 1), :])
        left = jnp.concatenate(parts, 0)
        high = left.astype(jnp.bfloat16)
        low = (left - high.astype(jnp.float32)).astype(jnp.bfloat16)
        wz = wz_ref[pl.ds(pl.multiple_of(row * 8, 8), 8), :]
        zhigh = wz.astype(jnp.bfloat16)
        zlow = (wz - zhigh.astype(jnp.float32)).astype(jnp.bfloat16)
        lhs = jnp.concatenate([high, low, high], 1)
        rhs = jnp.concatenate([zhigh, zhigh, zlow], 1)
        rhs = jnp.concatenate([rhs, jnp.zeros((LANES - 8, 3 * LANES), jnp.bfloat16)], 0)
        return lax.dot_general(lhs, rhs, (((1,), (1,)), ((), ())), preferred_element_type=jnp.float32)

    def place(block, sums):
        base_x = 2 * lax.div(block, half_y * half_z)
        rest = lax.rem(block, half_y * half_z)
        base_y = lax.div(rest, half_z)
        base_z = lax.rem(rest, half_z)
        layer = jnp.where(base_z == 0, planes, jnp.where(base_z == half_z - 1, 2 * planes, 0))
        shift = lax.rem(2 * base_z + LANES - 1, LANES)
        sums = pltpu.roll(sums, shift, 1)
        at = pl.ds(pl.multiple_of(base_y * 8, 8), 16)
        for a in range(4):
            spot = layer + base_x + a
            grid_ref[spot, at, :] = grid_ref[spot, at, :] + sums[a * 16 : a * 16 + 16]

    def row_group(i, carry):
        results = [stencil(i * 8 + s) for s in range(8)]
        for s in range(8):
            place(block_ref[i * 8 + s], results[s])
        return carry

    lax.fori_loop(0, rows // 8, row_group, 0)

    def came_group(i, carry):
        results = [stencil(rows + i * 8 + s) for s in range(8)]
        for s in range(8):
            place(came_ref[i * 8 + s], results[s])
        return carry

    lax.fori_loop(0, came // 64, came_group, 0)

    def finish(i, carry):
        at = pl.ds(pl.multiple_of(i * 8, 8), 8)
        low, high = zero8, zero8
        for x in range(planes):
            first = grid_ref[planes + x, at, :]
            last = grid_ref[2 * planes + x, at, :]
            main = grid_ref[x, at, :] + jnp.where(lane < LANES - 1, first, 0.0) + jnp.where(lane > 0, last, 0.0)
            out_ref[x, at, :] = main
            low = jnp.where(lane == x, pltpu.roll(first, x + 1, 1), low)
            low = jnp.where(lane == 16 + x, pltpu.roll(main, 16 + x, 1), low)
            high = jnp.where(lane == x, pltpu.roll(last, x, 1) if x else last, high)
            high = jnp.where(lane == 16 + x, pltpu.roll(main, 17 + x, 1), high)
        out_ref[planes, at, :] = low
        out_ref[planes + 1, at, :] = high
        return carry

    lax.fori_loop(0, out_ref.shape[1] // 8, finish, 0)


def halo_kernel(counts, grid_in, out_ref, z_box, y_box, x_box, edge_ref, edge_box, send_sem, recv_sem):
    planes = out_ref.shape[0] - 2
    tall = out_ref.shape[1]
    sides = neighbours(counts)
    lane = lax.broadcasted_iota(jnp.int32, (8, LANES), 1)
    z_box[...] = jnp.zeros_like(z_box)
    y_box[...] = jnp.zeros_like(y_box)
    x_box[...] = jnp.zeros_like(x_box)
    edge_box[...] = jnp.zeros_like(edge_box)
    greet(sides)

    def exchange(ways, sources, targets, sems):
        copies = []
        for way, source, target_ref, sem in zip(ways, sources, targets, sems):
            axis, target, there, other = sides[way]
            copy = remote(source, target_ref, send_sem.at[sem], recv_sem.at[sem], axis, target)
            pl.when(there)(copy.start)
            copies.append((copy, there, other))
        for copy, there, other in copies:
            pl.when(there)(copy.wait_send)
            pl.when(other)(copy.wait_recv)

    exchange((4, 5), (grid_in.at[planes], grid_in.at[planes + 1]), (z_box.at[0], z_box.at[1]), (4, 5))

    def add_z(i, carry):
        at = pl.ds(pl.multiple_of(i * 8, 8), 8)
        above, below = z_box[0, at, :], z_box[1, at, :]
        for x in range(planes):
            main = grid_in[x, at, :]
            main = main + jnp.where(lane == LANES - 1, pltpu.roll(above, LANES - 1 - x, 1), 0.0)
            down = pltpu.roll(below, LANES - x, 1) if x else below
            out_ref[x, at, :] = main + jnp.where(lane == 0, down, 0.0)
        out_ref[planes, at, :] = grid_in[planes, at, :] + pltpu.roll(below, LANES - 16, 1)
        out_ref[planes + 1, at, :] = grid_in[planes + 1, at, :] + pltpu.roll(above, LANES - 16, 1)
        return carry

    lax.fori_loop(0, tall // 8, add_z, 0)
    first, last = pl.ds(0, 8), pl.ds(tall - 8, 8)
    exchange(
        (2, 3),
        (out_ref.at[:, first, :], out_ref.at[:, last, :]),
        (y_box.at[0], y_box.at[1]),
        (2, 3),
    )
    for x in range(planes + 2):
        out_ref[x, last, :] = out_ref[x, last, :] + y_box[0, x]
        out_ref[x, first, :] = out_ref[x, first, :] + y_box[1, x]

    def pack(i, carry):
        at = pl.ds(pl.multiple_of(i * 8, 8), 8)
        edge_ref[at, :] = jnp.where(lane < 16, out_ref[planes, at, :], pltpu.roll(out_ref[planes + 1, at, :], 16, 1))
        return carry

    lax.fori_loop(0, tall // 8, pack, 0)
    exchange(
        (0, 1, 0, 1),
        (out_ref.at[pl.ds(0, 2)], out_ref.at[pl.ds(planes - 2, 2)], edge_ref, edge_ref),
        (x_box.at[0], x_box.at[1], edge_box.at[0], edge_box.at[1]),
        (0, 1, 6, 7),
    )

    def add_x(i, carry):
        at = pl.ds(pl.multiple_of(i * 8, 8), 8)
        for p in range(2):
            out_ref[planes - 2 + p, at, :] = out_ref[planes - 2 + p, at, :] + x_box[0, p, at, :]
            out_ref[p, at, :] = out_ref[p, at, :] + x_box[1, p, at, :]
        above, below = edge_box[0, at, :], edge_box[1, at, :]
        for side in range(2):
            value = out_ref[planes + side, at, :]
            start = 16 * side
            value = value + jnp.where(
                lane == planes - 2, pltpu.roll(above, (planes - 2 - start) % LANES, 1), 0.0
            )
            value = value + jnp.where(
                lane == 1, pltpu.roll(below, (1 - (planes - 1) - start) % LANES, 1), 0.0
            )
            out_ref[planes + side, at, :] = value
        return carry

    lax.fori_loop(0, tall // 8, add_x, 0)


def update_kernel(counts, grid_ref, mat_ref, stiff_ref, mass_ref, vel_ref, v_ref, z_ref):
    span_x, span_y, span_z = mass_ref.shape
    planes = span_x + 2
    there = [side[2].astype(jnp.float32) for side in neighbours(counts)]
    lane = lax.broadcasted_iota(jnp.int32, (span_y, LANES), 1)
    bottom = jnp.logical_and(lane == 0, jnp.logical_not(lax.axis_index("gz") > 0))

    def speeds(x, start, length, scale):
        def read(k):
            if length == 1:
                return grid_ref[x, pl.ds(start * 4 + k, 1), :]
            return grid_ref[x, pl.ds(start * 4 + k, length, stride=4), :]

        under = scale / jnp.maximum(read(0), 1.0)
        return [read(1 + j) * under for j in range(3)]

    def fill(x, carry):
        scale = jnp.where(x == 0, there[0], jnp.where(x == planes - 1, there[1], 1.0))
        for j, value in enumerate(speeds(x, 1, span_y, scale)):
            v_ref[j, x, pl.ds(8, span_y), :] = value
        for j, value in enumerate(speeds(x, 0, 1, there[2])):
            v_ref[j, x, pl.ds(7, 1), :] = value
        for j, value in enumerate(speeds(x, span_y + 1, 1, there[3])):
            v_ref[j, x, pl.ds(8 + span_y, 1), :] = value
        return carry

    lax.fori_loop(0, planes, fill, 0)
    for side in range(2):
        for j, value in enumerate(speeds(planes + side, 1, span_y, there[4 + side])):
            z_ref[side, j] = value

    def update(x, carry):
        mass_ref[x] = grid_ref[x + 1, pl.ds(4, span_y, stride=4), :]
        material = mat_ref[x]
        stiff = jnp.zeros((span_y, LANES), jnp.float32)
        for m in range(stiff_ref.shape[0]):
            stiff = jnp.where(material == m, stiff_ref[m], stiff)
        for j in range(3):
            value = v_ref[j, x + 1, pl.ds(8, span_y), :]
            beside = v_ref[j, x + 2, pl.ds(8, span_y), :] + v_ref[j, x, pl.ds(8, span_y), :]
            beside = beside + v_ref[j, x + 1, pl.ds(9, span_y), :] + v_ref[j, x + 1, pl.ds(7, span_y), :]
            after = pltpu.roll(z_ref[1, j], LANES - 2 - x, 1)
            before = pltpu.roll(z_ref[0, j], LANES - 1 - x, 1)
            beside = beside + jnp.where(lane == LANES - 1, after, pltpu.roll(value, LANES - 1, 1))
            beside = beside + jnp.where(lane == 0, before, pltpu.roll(value, 1, 1))
            result = value + stiff * (beside - 6.0 * value)
            if j == 2:
                result = result - gravity_step
                result = jnp.where(bottom, jnp.maximum(result, 0.0), result)
            vel_ref[j, x] = result
        return carry

    lax.fori_loop(0, span_x, update, 0)


def per_device(
    counts, row_owner, row_count, row_block, offsets, particle_mass, particle_velocity, material, stiffness
):
    rows = particle_mass.shape[0]
    span_x, span_y, span_z = material.shape
    planes = span_x + 2
    tall = (span_y + 2) * 4
    f32 = jnp.float32
    vmem = pl.BlockSpec(memory_space=pltpu.VMEM)
    smem = pl.BlockSpec(memory_space=pltpu.SMEM)
    myself = (lax.axis_index("gx") * counts["gy"] + lax.axis_index("gy")) * counts["gz"] + lax.axis_index("gz")

    box = pl.pallas_call(
        functools.partial(rows_kernel, counts),
        out_shape=jax.ShapeDtypeStruct((6, CAP, 8, LANES), f32),
        in_specs=[vmem, smem, smem, vmem, vmem, vmem],
        out_specs=vmem,
        scratch_shapes=[
            pltpu.VMEM((6, CAP, 8, LANES), f32),
            pltpu.SemaphoreType.DMA((6,)),
            pltpu.SemaphoreType.DMA((6,)),
        ],
        compiler_params=pltpu.CompilerParams(
            collective_id=0, has_side_effects=True, vmem_limit_bytes=VMEM_LIMIT
        ),
        name="row_exchange",
    )(row_owner.reshape(-1, LANES), row_count, row_block, offsets, particle_mass, particle_velocity)

    came_blocks = box[:, :, 7, 0].reshape(-1).astype(jnp.int32)
    total = rows + 6 * CAP
    grid = pl.pallas_call(
        functools.partial(deposit_kernel, span_y // 2, span_z // 2, planes),
        out_shape=jax.ShapeDtypeStruct((planes + 2, tall, LANES), f32),
        in_specs=[smem] * 5 + [vmem] * 4,
        out_specs=vmem,
        scratch_shapes=[
            pltpu.VMEM((3 * planes, tall, LANES), f32),
            pltpu.VMEM((total * 4, LANES), f32),
            pltpu.VMEM((total * 16, LANES), f32),
            pltpu.VMEM((total * 8, LANES), f32),
        ],
        compiler_params=pltpu.CompilerParams(vmem_limit_bytes=VMEM_LIMIT),
        name="deposit",
    )(
        myself.reshape(1), row_owner, row_count, row_block, came_blocks,
        offsets, particle_mass, particle_velocity, box.reshape(6 * CAP * 8, LANES),
    )

    grid = pl.pallas_call(
        functools.partial(halo_kernel, counts),
        out_shape=jax.ShapeDtypeStruct((planes + 2, tall, LANES), f32),
        in_specs=[vmem],
        out_specs=vmem,
        scratch_shapes=[
            pltpu.VMEM((2, tall, LANES), f32),
            pltpu.VMEM((2, planes + 2, 8, LANES), f32),
            pltpu.VMEM((2, 2, tall, LANES), f32),
            pltpu.VMEM((tall, LANES), f32),
            pltpu.VMEM((2, tall, LANES), f32),
            pltpu.SemaphoreType.DMA((8,)),
            pltpu.SemaphoreType.DMA((8,)),
        ],
        compiler_params=pltpu.CompilerParams(
            collective_id=1, has_side_effects=True, vmem_limit_bytes=VMEM_LIMIT
        ),
        name="halo_sums",
    )(grid)

    return pl.pallas_call(
        functools.partial(update_kernel, counts),
        out_shape=(
            jax.ShapeDtypeStruct((span_x, span_y, span_z), f32),
            jax.ShapeDtypeStruct((3, span_x, span_y, span_z), f32),
        ),
        in_specs=[vmem, vmem, smem],
        out_specs=(vmem, vmem),
        scratch_shapes=[
            pltpu.VMEM((3, planes, span_y + 16, LANES), f32),
            pltpu.VMEM((2, 3, span_y, LANES), f32),
        ],
        compiler_params=pltpu.CompilerParams(vmem_limit_bytes=VMEM_LIMIT),
        name="grid_update",
    )(grid, material, stiffness)


def solution(mesh):
    placed = (
        P(("runs", "gx", "gy", "gz")),
        P(("runs", "gx", "gy", "gz")),
        P(("runs", "gx", "gy", "gz")),
        P(None, ("runs", "gx", "gy", "gz"), None),
        P(("runs", "gx", "gy", "gz"), None),
        P(None, ("runs", "gx", "gy", "gz"), None),
        P(("runs", "gx"), "gy", "gz"),
        P(),
    )
    counts = {axis: mesh.shape[axis] for axis in AXES}
    return jax.shard_map(
        functools.partial(per_device, counts),
        mesh=mesh,
        in_specs=placed,
        out_specs=(P(("runs", "gx"), "gy", "gz"), P(None, ("runs", "gx"), "gy", "gz")),
        check_vma=False,
    )
```

```python
import functools

import jax
import jax.numpy as jnp
from jax import lax
from jax.experimental import pallas as pl
from jax.experimental.pallas import tpu as pltpu
from jax.sharding import PartitionSpec as P

CAP = 4
LANES = 128
gravity_step = 0.05
AXES = ("gx", "gy", "gz")
VMEM_LIMIT = 48 * 1024 * 1024


def spline(distance):
    distance = jnp.abs(distance)
    inside_part = 0.75 - distance * distance
    rest = jnp.maximum(1.5 - distance, 0.0)
    return jnp.where(distance < 0.5, inside_part, 0.5 * rest * rest)


def neighbours(counts):
    found = []
    for axis in AXES:
        here = lax.axis_index(axis)
        low = here > 0
        high = here < counts[axis] - 1
        found.append((axis, here - 1, low, high))
        found.append((axis, here + 1, high, low))
    return found


def greet(sides):
    barrier = pltpu.get_barrier_semaphore()
    total = 0
    for axis, target, there, _ in sides:
        @pl.when(there)
        def _():
            pl.semaphore_signal(
                barrier, inc=1, device_id={axis: target}, device_id_type=pl.DeviceIdType.MESH
            )
        total = total + there.astype(jnp.int32)
    return lambda: pl.semaphore_wait(barrier, total)


def load(sources, targets, sems):
    copies = [pltpu.make_async_copy(s, t, sems.at[n]) for n, (s, t) in enumerate(zip(sources, targets))]
    for copy in copies:
        copy.start()
    return copies


def remote(source, target_ref, send_sem, recv_sem, axis, target):
    return pltpu.make_async_remote_copy(
        src_ref=source,
        dst_ref=target_ref,
        send_sem=send_sem,
        recv_sem=recv_sem,
        device_id={axis: target},
        device_id_type=pl.DeviceIdType.MESH,
    )


def rows_kernel(
    counts, owner_in, count_in, block_in, offs_in, mass_in, vel_in, box_ref,
    owner_ref, count_ref, block_ref, offs_ref, mass_ref, vel_ref, out_box, load_sem, send_sem, recv_sem,
):
    loads = load(
        (owner_in, count_in, block_in, offs_in, mass_in, vel_in),
        (owner_ref, count_ref, block_ref, offs_ref, mass_ref, vel_ref),
        load_sem,
    )
    rows = mass_ref.shape[0]
    size_y, size_z = counts["gy"], counts["gz"]
    myself = (lax.axis_index("gx") * size_y + lax.axis_index("gy")) * size_z + lax.axis_index("gz")
    sides = neighbours(counts)
    box_ref[...] = jnp.zeros_like(box_ref)
    greeted = greet(sides)
    loads[0].wait()
    heading = owner_ref[...] - myself
    shape = heading.shape
    place = lax.broadcasted_iota(jnp.int32, shape, 0) * LANES + lax.broadcasted_iota(jnp.int32, shape, 1)
    lane = lax.broadcasted_iota(jnp.int32, (1, LANES), 1)
    steps = (-size_y * size_z, size_y * size_z, -size_z, size_z, -1, 1)
    left = [jnp.where(heading == step, place, rows) for step in steps]
    for copy in loads[1:]:
        copy.wait()
    for slot in range(CAP):
        for way in range(6):
            first = jnp.min(left[way])
            left[way] = jnp.where(left[way] == first, rows, left[way])
            valid = first < rows
            row = jnp.minimum(first, rows - 1)
            live = jnp.where(valid, count_ref[row], 0)
            for j in range(3):
                out_box[way, slot, pl.ds(j, 1), :] = offs_ref[j, pl.ds(row, 1), :]
                out_box[way, slot, pl.ds(4 + j, 1), :] = vel_ref[j, pl.ds(row, 1), :]
            out_box[way, slot, pl.ds(3, 1), :] = jnp.where(lane < live, mass_ref[pl.ds(row, 1), :], 0.0)
            block = jnp.where(valid, block_ref[row], 0).astype(jnp.float32)
            out_box[way, slot, pl.ds(7, 1), :] = jnp.full((1, LANES), block, jnp.float32)
    greeted()
    copies = [
        remote(out_box.at[way], box_ref.at[way], send_sem.at[way], recv_sem.at[way], axis, target)
        for way, (axis, target, _, _) in enumerate(sides)
    ]
    for way, (_, _, there, _) in enumerate(sides):
        pl.when(there)(copies[way].start)
    for way, (_, _, there, other) in enumerate(sides):
        pl.when(there)(copies[way].wait_send)
        pl.when(other)(copies[way].wait_recv)


def deposit_kernel(
    half_y, half_z, planes, me_ref, came_ref, owner_in, count_in, block_in, offs_in, mass_in, vel_in,
    box_ref, out_ref, owner_ref, count_ref, block_ref, offs_ref, mass_ref, vel_ref, load_sem,
    grid_ref, wx_ref, yk_ref, wz_ref, even_ref, odd_ref,
):
    loads = load(
        (owner_in, count_in, block_in, offs_in, mass_in, vel_in),
        (owner_ref, count_ref, block_ref.at[pl.ds(0, mass_ref.shape[0])], offs_ref, mass_ref, vel_ref),
        load_sem,
    )
    rows = mass_ref.shape[0]
    came = box_ref.shape[0]
    total = block_ref.shape[0]
    row_half = even_ref.shape[0]
    sub = lax.broadcasted_iota(jnp.int32, (8, LANES), 0)
    lane = lax.broadcasted_iota(jnp.int32, (8, LANES), 1)
    myself = me_ref[0]
    zero8 = jnp.zeros((8, LANES), jnp.float32)

    def clear(i, carry):
        grid_ref[i] = jnp.zeros(grid_ref.shape[1:], jnp.float32)
        return carry

    lax.fori_loop(0, grid_ref.shape[0], clear, 0)
    for copy in loads:
        copy.wait()

    def fill(base, ox, oy, oz, carried):
        for a in range(4):
            wx_ref[pl.ds(base * 4 + a, 8, stride=4), :] = spline(ox + (0.5 - a))
            wy = spline(oy + (0.5 - a))
            for k in range(4):
                yk_ref[pl.ds(base * 16 + a * 4 + k, 8, stride=16), :] = wy * carried[k]
            wz_ref[pl.ds(base * 8 + a, 8, stride=8), :] = spline(oz + (0.5 - a))
            wz_ref[pl.ds(base * 8 + 4 + a, 8, stride=8), :] = zero8

    def prepare(i, carry):
        base = pl.multiple_of(i * 8, 8)
        live = jnp.zeros((8, LANES), jnp.int32)
        for s in range(8):
            count = jnp.where(owner_ref[base + s] == myself, count_ref[base + s], 0)
            live = jnp.where(sub == s, count, live)
        at = pl.ds(base, 8)
        mass = jnp.where(lane < live, mass_ref[at, :], 0.0)
        carried = [mass] + [mass * vel_ref[j, at, :] for j in range(3)]
        fill(base, offs_ref[0, at, :], offs_ref[1, at, :], offs_ref[2, at, :], carried)
        return carry

    lax.fori_loop(0, rows // 8, prepare, 0)
    for group in range(came // 64):
        part = [box_ref[pl.ds(group * 64 + c, 8, stride=8), :] for c in range(8)]
        carried = [part[3]] + [part[3] * part[4 + j] for j in range(3)]
        fill(rows + group * 8, part[0], part[1], part[2], carried)
    for group in range(rows + came // 8, total, 8):
        fill(group, zero8, zero8, zero8, [zero8] * 4)
    for row in range(rows, total):
        block_ref[row] = came_ref[row - rows] if row < rows + came // 8 else 0

    def stencil(row):
        parts = []
        yk = yk_ref[pl.ds(pl.multiple_of(row * 16, 16), 16), :]
        for a in range(4):
            parts.append(yk * wx_ref[pl.ds(row * 4 + a, 1), :])
        left = jnp.concatenate(parts, 0)
        high = left.astype(jnp.bfloat16)
        low = (left - high.astype(jnp.float32)).astype(jnp.bfloat16)
        wz = wz_ref[pl.ds(pl.multiple_of(row * 8, 8), 8), :]
        zhigh = wz.astype(jnp.bfloat16)
        zlow = (wz - zhigh.astype(jnp.float32)).astype(jnp.bfloat16)
        lhs = jnp.concatenate([high, low, high], 1)
        rhs = jnp.concatenate([zhigh, zhigh, zlow], 1)
        rhs = jnp.concatenate([rhs, jnp.zeros((LANES - 8, 3 * LANES), jnp.bfloat16)], 0)
        return lax.dot_general(lhs, rhs, (((1,), (1,)), ((), ())), preferred_element_type=jnp.float32)

    def place(block, sums):
        base_x = 2 * lax.div(block, half_y * half_z)
        rest = lax.rem(block, half_y * half_z)
        base_y = lax.div(rest, half_z)
        base_z = lax.rem(rest, half_z)
        layer = jnp.where(base_z == 0, planes, jnp.where(base_z == half_z - 1, 2 * planes, 0))
        shift = lax.rem(2 * base_z + LANES - 1, LANES)
        sums = pltpu.roll(sums, shift, 1)
        at = pl.ds(pl.multiple_of(base_y * 8, 8), 16)
        for a in range(4):
            spot = layer + base_x + a
            grid_ref[spot, at, :] = grid_ref[spot, at, :] + sums[a * 16 : a * 16 + 16]

    half = row_half
    even_ref[...] = jnp.zeros(even_ref.shape, jnp.float32)
    odd_ref[...] = jnp.zeros(odd_ref.shape, jnp.float32)

    def row_group(i, carry):
        base = i * 2 * half
        for s in range(half):
            even_ref[s] = stencil(base + s)
        for s in range(half):
            place(block_ref[jnp.maximum(base - half + s, 0)], odd_ref[s])
        for s in range(half):
            odd_ref[s] = stencil(base + half + s)
        for s in range(half):
            place(block_ref[base + s], even_ref[s])
        return carry

    lax.fori_loop(0, total // (2 * half), row_group, 0)
    for s in range(half):
        place(block_ref[total - half + s], odd_ref[s])

    def finish(i, carry):
        at = pl.ds(pl.multiple_of(i * 8, 8), 8)
        low, high = zero8, zero8
        for x in range(planes):
            first = grid_ref[planes + x, at, :]
            last = grid_ref[2 * planes + x, at, :]
            main = grid_ref[x, at, :] + jnp.where(lane < LANES - 1, first, 0.0) + jnp.where(lane > 0, last, 0.0)
            out_ref[x, at, :] = main
            low = jnp.where(lane == x, pltpu.roll(first, x + 1, 1), low)
            low = jnp.where(lane == 16 + x, pltpu.roll(main, 16 + x, 1), low)
            high = jnp.where(lane == x, pltpu.roll(last, x, 1) if x else last, high)
            high = jnp.where(lane == 16 + x, pltpu.roll(main, 17 + x, 1), high)
        out_ref[planes, at, :] = low
        out_ref[planes + 1, at, :] = high
        return carry

    lax.fori_loop(0, out_ref.shape[1] // 8, finish, 0)


def halo_kernel(
    counts, grid_in, out_ref, z_box, y_box, x_box, c_box, edge_ref, e_out, e_box, col_ref, send_sem, recv_sem
):
    planes = out_ref.shape[0] - 2
    tall = out_ref.shape[1]
    chunks = tall // 8
    blocks = edge_ref.shape[0] // LANES
    sides = neighbours(counts)
    lane = lax.broadcasted_iota(jnp.int32, (8, LANES), 1)
    for box in (z_box, y_box, x_box, c_box, e_box):
        box[...] = jnp.zeros_like(box)
    greet(sides)()
    first, last = pl.ds(0, 8), pl.ds(tall - 8, 8)

    def begin(way, source, target_ref, sem):
        axis, target, there, other = sides[way]
        copy = remote(source, target_ref, send_sem.at[sem], recv_sem.at[sem], axis, target)
        pl.when(there)(copy.start)
        return copy, there, other

    def end(copies):
        for copy, there, other in copies:
            pl.when(there)(copy.wait_send)
            pl.when(other)(copy.wait_recv)

    def roll(value, shift):
        shift = shift % LANES
        return pltpu.roll(value, shift, 1) if shift else value

    bulk = [
        begin(0, grid_in.at[pl.ds(0, 2)], x_box.at[0], 0),
        begin(1, grid_in.at[pl.ds(planes - 2, 2)], x_box.at[1], 1),
    ]
    end([
        begin(4, grid_in.at[planes], z_box.at[0], 4),
        begin(5, grid_in.at[planes + 1], z_box.at[1], 5),
    ])

    def add_z(i, carry):
        at = pl.ds(i * 8 if isinstance(i, int) else pl.multiple_of(i * 8, 8), 8)
        above, below = z_box[0, at, :], z_box[1, at, :]
        for x in range(planes):
            main = grid_in[x, at, :]
            main = main + jnp.where(lane == LANES - 1, roll(above, LANES - 1 - x), 0.0)
            out_ref[x, at, :] = main + jnp.where(lane == 0, roll(below, -x), 0.0)
        out_ref[planes, at, :] = grid_in[planes, at, :] + roll(below, -16)
        out_ref[planes + 1, at, :] = grid_in[planes + 1, at, :] + roll(above, -16)
        return carry

    add_z(0, 0)
    add_z(chunks - 1, 0)
    across = [
        begin(2, out_ref.at[:, first, :], y_box.at[0], 2),
        begin(3, out_ref.at[:, last, :], y_box.at[1], 3),
    ]
    lax.fori_loop(1, chunks - 1, add_z, 0)
    end(across)
    corner = [
        begin(0, y_box.at[:, pl.ds(0, 2)], c_box.at[0], 6),
        begin(1, y_box.at[:, pl.ds(planes - 2, 2)], c_box.at[1], 7),
    ]
    for x in range(planes + 2):
        out_ref[x, last, :] = out_ref[x, last, :] + y_box[0, x]
        out_ref[x, first, :] = out_ref[x, first, :] + y_box[1, x]

    def pack(i, carry):
        at = pl.ds(pl.multiple_of(i * 8, 8), 8)
        zlow, zhigh = out_ref[planes, at, :], out_ref[planes + 1, at, :]
        above, below = z_box[0, at, :], z_box[1, at, :]
        value = jnp.where(lane == 0, zlow, jnp.where(lane == 1, roll(zhigh, 1), 0.0))
        value = jnp.where(lane == 8, roll(zlow, 8 - (planes - 1)), value)
        value = jnp.where(lane == 9, roll(zhigh, 9 - (planes - 1)), value)
        value = jnp.where((lane == 2) | (lane == 3), roll(above, 2), value)
        value = jnp.where((lane == 4) | (lane == 5), roll(below, 4), value)
        value = jnp.where((lane == 10) | (lane == 11), roll(above, 10 - (planes - 2)), value)
        value = jnp.where((lane == 12) | (lane == 13), roll(below, 12 - (planes - 2)), value)
        edge_ref[at, :] = value
        return carry

    lax.fori_loop(0, chunks, pack, 0)
    edge_ref[pl.ds(tall, blocks * LANES - tall), :] = jnp.zeros((blocks * LANES - tall, LANES), jnp.float32)
    for block in range(blocks):
        at = pl.ds(block * LANES, LANES)
        turned = jnp.transpose(edge_ref[at, :])
        e_out[0, :, at] = turned[0:8]
        e_out[1, :, at] = turned[8:16]
    corner = corner + [begin(0, e_out.at[0], e_box.at[0], 8), begin(1, e_out.at[1], e_box.at[1], 9)]
    end(bulk)
    end(corner)
    for block in range(blocks):
        at = pl.ds(block * LANES, LANES)
        both = jnp.concatenate(
            [e_box[0, :, at], e_box[1, :, at], jnp.zeros((LANES - 16, LANES), jnp.float32)], 0
        )
        col_ref[at, :] = jnp.transpose(both)
    for p in range(2):
        high, low = planes - 2 + p, p
        out_ref[high, last, :] = out_ref[high, last, :] + c_box[0, 0, p]
        out_ref[high, first, :] = out_ref[high, first, :] + c_box[0, 1, p]
        out_ref[low, last, :] = out_ref[low, last, :] + c_box[1, 0, p]
        out_ref[low, first, :] = out_ref[low, first, :] + c_box[1, 1, p]

    def add_x(i, carry):
        at = pl.ds(pl.multiple_of(i * 8, 8), 8)
        col = col_ref[at, :]

        def put(spot, source):
            return jnp.where(lane == spot, roll(col, spot - source), 0.0)

        for p in range(2):
            high, low = planes - 2 + p, p
            out_ref[high, at, :] = (
                out_ref[high, at, :] + x_box[0, p, at, :] + put(LANES - 1, 2 + p) + put(0, 4 + p)
            )
            out_ref[low, at, :] = (
                out_ref[low, at, :] + x_box[1, p, at, :] + put(LANES - 1, 10 + p) + put(0, 12 + p)
            )
        for side in range(2):
            out_ref[planes + side, at, :] = (
                out_ref[planes + side, at, :] + put(planes - 2, side) + put(1, 8 + side)
            )
        return carry

    lax.fori_loop(0, chunks, add_x, 0)


def update_kernel(counts, grid_ref, mat_ref, stiff_ref, mass_ref, vel_ref, v_ref, z_ref):
    span_x, span_y, span_z = mass_ref.shape
    planes = span_x + 2
    there = [side[2].astype(jnp.float32) for side in neighbours(counts)]
    lane = lax.broadcasted_iota(jnp.int32, (span_y, LANES), 1)
    bottom = jnp.logical_and(lane == 0, jnp.logical_not(lax.axis_index("gz") > 0))

    def speeds(x, start, length, scale):
        def read(k):
            if length == 1:
                return grid_ref[x, pl.ds(start * 4 + k, 1), :]
            return grid_ref[x, pl.ds(start * 4 + k, length, stride=4), :]

        under = scale / jnp.maximum(read(0), 1.0)
        return [read(1 + j) * under for j in range(3)]

    def fill(x, carry):
        scale = jnp.where(x == 0, there[0], jnp.where(x == planes - 1, there[1], 1.0))
        for j, value in enumerate(speeds(x, 1, span_y, scale)):
            v_ref[j, x, pl.ds(8, span_y), :] = value
        for j, value in enumerate(speeds(x, 0, 1, there[2])):
            v_ref[j, x, pl.ds(7, 1), :] = value
        for j, value in enumerate(speeds(x, span_y + 1, 1, there[3])):
            v_ref[j, x, pl.ds(8 + span_y, 1), :] = value
        return carry

    lax.fori_loop(0, planes, fill, 0)
    for side in range(2):
        for j, value in enumerate(speeds(planes + side, 1, span_y, there[4 + side])):
            z_ref[side, j] = value

    def update(x, carry):
        mass_ref[x] = grid_ref[x + 1, pl.ds(4, span_y, stride=4), :]
        material = mat_ref[x]
        stiff = jnp.zeros((span_y, LANES), jnp.float32)
        for m in range(stiff_ref.shape[0]):
            stiff = jnp.where(material == m, stiff_ref[m], stiff)
        for j in range(3):
            value = v_ref[j, x + 1, pl.ds(8, span_y), :]
            beside = v_ref[j, x + 2, pl.ds(8, span_y), :] + v_ref[j, x, pl.ds(8, span_y), :]
            beside = beside + v_ref[j, x + 1, pl.ds(9, span_y), :] + v_ref[j, x + 1, pl.ds(7, span_y), :]
            after = pltpu.roll(z_ref[1, j], LANES - 2 - x, 1)
            before = pltpu.roll(z_ref[0, j], LANES - 1 - x, 1)
            beside = beside + jnp.where(lane == LANES - 1, after, pltpu.roll(value, LANES - 1, 1))
            beside = beside + jnp.where(lane == 0, before, pltpu.roll(value, 1, 1))
            result = value + stiff * (beside - 6.0 * value)
            if j == 2:
                result = result - gravity_step
                result = jnp.where(bottom, jnp.maximum(result, 0.0), result)
            vel_ref[j, x] = result
        return carry

    lax.fori_loop(0, span_x, update, 0)


def per_device(
    counts, row_owner, row_count, row_block, offsets, particle_mass, particle_velocity, material, stiffness
):
    rows = particle_mass.shape[0]
    span_x, span_y, span_z = material.shape
    planes = span_x + 2
    tall = (span_y + 2) * 4
    wide = pl.cdiv(tall, LANES) * LANES
    f32 = jnp.float32
    vmem = pl.BlockSpec(memory_space=pltpu.VMEM)
    hbm = pl.BlockSpec(memory_space=pl.ANY)
    smem = pl.BlockSpec(memory_space=pltpu.SMEM)
    myself = (lax.axis_index("gx") * counts["gy"] + lax.axis_index("gy")) * counts["gz"] + lax.axis_index("gz")

    box = pl.pallas_call(
        functools.partial(rows_kernel, counts),
        out_shape=jax.ShapeDtypeStruct((6, CAP, 8, LANES), f32),
        in_specs=[hbm] * 6,
        out_specs=vmem,
        scratch_shapes=[
            pltpu.VMEM((rows // LANES, LANES), jnp.int32),
            pltpu.SMEM((rows,), jnp.int32),
            pltpu.SMEM((rows,), jnp.int32),
            pltpu.VMEM(offsets.shape, f32),
            pltpu.VMEM(particle_mass.shape, f32),
            pltpu.VMEM(particle_velocity.shape, f32),
            pltpu.VMEM((6, CAP, 8, LANES), f32),
            pltpu.SemaphoreType.DMA((6,)),
            pltpu.SemaphoreType.DMA((6,)),
            pltpu.SemaphoreType.DMA((6,)),
        ],
        compiler_params=pltpu.CompilerParams(
            collective_id=0, has_side_effects=True, vmem_limit_bytes=VMEM_LIMIT
        ),
        name="row_exchange",
    )(row_owner.reshape(-1, LANES), row_count, row_block, offsets, particle_mass, particle_velocity)

    came_blocks = box[:, :, 7, 0].reshape(-1).astype(jnp.int32)
    half = 8
    total = pl.cdiv(rows + 6 * CAP, 2 * half) * 2 * half
    grid = pl.pallas_call(
        functools.partial(deposit_kernel, span_y // 2, span_z // 2, planes),
        out_shape=jax.ShapeDtypeStruct((planes + 2, tall, LANES), f32),
        in_specs=[smem] * 2 + [hbm] * 6 + [vmem],
        out_specs=vmem,
        scratch_shapes=[
            pltpu.SMEM((rows,), jnp.int32),
            pltpu.SMEM((rows,), jnp.int32),
            pltpu.SMEM((total,), jnp.int32),
            pltpu.VMEM(offsets.shape, f32),
            pltpu.VMEM(particle_mass.shape, f32),
            pltpu.VMEM(particle_velocity.shape, f32),
            pltpu.SemaphoreType.DMA((6,)),
            pltpu.VMEM((3 * planes, tall, LANES), f32),
            pltpu.VMEM((total * 4, LANES), f32),
            pltpu.VMEM((total * 16, LANES), f32),
            pltpu.VMEM((total * 8, LANES), f32),
            pltpu.VMEM((half, 64, LANES), f32),
            pltpu.VMEM((half, 64, LANES), f32),
        ],
        compiler_params=pltpu.CompilerParams(vmem_limit_bytes=VMEM_LIMIT),
        name="deposit",
    )(
        myself.reshape(1), came_blocks, row_owner, row_count, row_block,
        offsets, particle_mass, particle_velocity, box.reshape(6 * CAP * 8, LANES),
    )

    grid = pl.pallas_call(
        functools.partial(halo_kernel, counts),
        out_shape=jax.ShapeDtypeStruct((planes + 2, tall, LANES), f32),
        in_specs=[vmem],
        out_specs=vmem,
        scratch_shapes=[
            pltpu.VMEM((2, tall, LANES), f32),
            pltpu.VMEM((2, planes + 2, 8, LANES), f32),
            pltpu.VMEM((2, 2, tall, LANES), f32),
            pltpu.VMEM((2, 2, 2, 8, LANES), f32),
            pltpu.VMEM((wide, LANES), f32),
            pltpu.VMEM((2, 8, wide), f32),
            pltpu.VMEM((2, 8, wide), f32),
            pltpu.VMEM((wide, LANES), f32),
            pltpu.SemaphoreType.DMA((10,)),
            pltpu.SemaphoreType.DMA((10,)),
        ],
        compiler_params=pltpu.CompilerParams(
            collective_id=1, has_side_effects=True, vmem_limit_bytes=VMEM_LIMIT
        ),
        name="halo_sums",
    )(grid)

    return pl.pallas_call(
        functools.partial(update_kernel, counts),
        out_shape=(
            jax.ShapeDtypeStruct((span_x, span_y, span_z), f32),
            jax.ShapeDtypeStruct((3, span_x, span_y, span_z), f32),
        ),
        in_specs=[vmem, vmem, smem],
        out_specs=(vmem, vmem),
        scratch_shapes=[
            pltpu.VMEM((3, planes, span_y + 16, LANES), f32),
            pltpu.VMEM((2, 3, span_y, LANES), f32),
        ],
        compiler_params=pltpu.CompilerParams(vmem_limit_bytes=VMEM_LIMIT),
        name="grid_update",
    )(grid, material, stiffness)


def solution(mesh):
    placed = (
        P(("runs", "gx", "gy", "gz")),
        P(("runs", "gx", "gy", "gz")),
        P(("runs", "gx", "gy", "gz")),
        P(None, ("runs", "gx", "gy", "gz"), None),
        P(("runs", "gx", "gy", "gz"), None),
        P(None, ("runs", "gx", "gy", "gz"), None),
        P(("runs", "gx"), "gy", "gz"),
        P(),
    )
    counts = {axis: mesh.shape[axis] for axis in AXES}
    return jax.shard_map(
        functools.partial(per_device, counts),
        mesh=mesh,
        in_specs=placed,
        out_specs=(P(("runs", "gx"), "gy", "gz"), P(None, ("runs", "gx"), "gy", "gz")),
        check_vma=False,
    )
```

```python
import functools

import jax
import jax.numpy as jnp
from jax import lax
from jax.experimental import pallas as pl
from jax.experimental.pallas import tpu as pltpu
from jax.sharding import PartitionSpec as P

CAP = 4
LANES = 128
gravity_step = 0.05
AXES = ("gx", "gy", "gz")
VMEM_LIMIT = 48 * 1024 * 1024
VMEM_WHOLE = 60 * 1024 * 1024


def spline(distance):
    distance = jnp.abs(distance)
    inside_part = 0.75 - distance * distance
    rest = jnp.maximum(1.5 - distance, 0.0)
    return jnp.where(distance < 0.5, inside_part, 0.5 * rest * rest)


def neighbours(counts):
    found = []
    for axis in AXES:
        here = lax.axis_index(axis)
        low = here > 0
        high = here < counts[axis] - 1
        found.append((axis, here - 1, low, high))
        found.append((axis, here + 1, high, low))
    return found


def greet(sides):
    barrier = pltpu.get_barrier_semaphore()
    total = 0
    for axis, target, there, _ in sides:
        @pl.when(there)
        def _():
            pl.semaphore_signal(
                barrier, inc=1, device_id={axis: target}, device_id_type=pl.DeviceIdType.MESH
            )
        total = total + there.astype(jnp.int32)
    return lambda: pl.semaphore_wait(barrier, total)


def load(sources, targets, sems):
    copies = [pltpu.make_async_copy(s, t, sems.at[n]) for n, (s, t) in enumerate(zip(sources, targets))]
    for copy in copies:
        copy.start()
    return copies


def remote(source, target_ref, send_sem, recv_sem, axis, target):
    return pltpu.make_async_remote_copy(
        src_ref=source,
        dst_ref=target_ref,
        send_sem=send_sem,
        recv_sem=recv_sem,
        device_id={axis: target},
        device_id_type=pl.DeviceIdType.MESH,
    )


def rows_kernel(
    counts, owner_in, count_in, block_in, offs_in, mass_in, vel_in, box_ref,
    owner_ref, count_ref, block_ref, offs_ref, mass_ref, vel_ref, out_box, load_sem, send_sem, recv_sem,
):
    loads = load(
        (owner_in, count_in, block_in, offs_in, mass_in, vel_in),
        (owner_ref, count_ref, block_ref, offs_ref, mass_ref, vel_ref),
        load_sem,
    )
    rows = mass_ref.shape[0]
    size_y, size_z = counts["gy"], counts["gz"]
    myself = (lax.axis_index("gx") * size_y + lax.axis_index("gy")) * size_z + lax.axis_index("gz")
    sides = neighbours(counts)
    box_ref[...] = jnp.zeros_like(box_ref)
    greeted = greet(sides)
    loads[0].wait()
    heading = owner_ref[...] - myself
    shape = heading.shape
    place = lax.broadcasted_iota(jnp.int32, shape, 0) * LANES + lax.broadcasted_iota(jnp.int32, shape, 1)
    lane = lax.broadcasted_iota(jnp.int32, (1, LANES), 1)
    steps = (-size_y * size_z, size_y * size_z, -size_z, size_z, -1, 1)
    left = [jnp.where(heading == step, place, rows) for step in steps]
    for copy in loads[1:]:
        copy.wait()
    for slot in range(CAP):
        for way in range(6):
            first = jnp.min(left[way])
            left[way] = jnp.where(left[way] == first, rows, left[way])
            valid = first < rows
            row = jnp.minimum(first, rows - 1)
            live = jnp.where(valid, count_ref[row], 0)
            for j in range(3):
                out_box[way, slot, pl.ds(j, 1), :] = offs_ref[j, pl.ds(row, 1), :]
                out_box[way, slot, pl.ds(4 + j, 1), :] = vel_ref[j, pl.ds(row, 1), :]
            out_box[way, slot, pl.ds(3, 1), :] = jnp.where(lane < live, mass_ref[pl.ds(row, 1), :], 0.0)
            block = jnp.where(valid, block_ref[row], 0).astype(jnp.float32)
            out_box[way, slot, pl.ds(7, 1), :] = jnp.full((1, LANES), block, jnp.float32)
    greeted()
    copies = [
        remote(out_box.at[way], box_ref.at[way], send_sem.at[way], recv_sem.at[way], axis, target)
        for way, (axis, target, _, _) in enumerate(sides)
    ]
    for way, (_, _, there, _) in enumerate(sides):
        pl.when(there)(copies[way].start)
    for way, (_, _, there, other) in enumerate(sides):
        pl.when(there)(copies[way].wait_send)
        pl.when(other)(copies[way].wait_recv)


def deposit_kernel(
    half_y, half_z, planes, me_ref, came_ref, owner_in, count_in, block_in, offs_in, mass_in, vel_in,
    box_ref, out_ref, owner_ref, count_ref, block_ref, offs_ref, mass_ref, vel_ref, load_sem,
    grid_ref, wx_ref, yk_ref, wz_ref, even_ref, odd_ref,
):
    loads = load(
        (owner_in, count_in, block_in, offs_in, mass_in, vel_in),
        (owner_ref, count_ref, block_ref.at[pl.ds(0, mass_ref.shape[0])], offs_ref, mass_ref, vel_ref),
        load_sem,
    )
    rows = mass_ref.shape[0]
    came = box_ref.shape[0]
    total = block_ref.shape[0]
    row_half = even_ref.shape[0]
    sub = lax.broadcasted_iota(jnp.int32, (8, LANES), 0)
    lane = lax.broadcasted_iota(jnp.int32, (8, LANES), 1)
    myself = me_ref[0]
    zero8 = jnp.zeros((8, LANES), jnp.float32)

    def clear(i, carry):
        grid_ref[i] = jnp.zeros(grid_ref.shape[1:], jnp.float32)
        return carry

    lax.fori_loop(0, grid_ref.shape[0], clear, 0)
    for copy in loads:
        copy.wait()

    def fill(base, ox, oy, oz, carried):
        for a in range(4):
            wx_ref[pl.ds(base * 4 + a, 8, stride=4), :] = spline(ox + (0.5 - a))
            wy = spline(oy + (0.5 - a))
            for k in range(4):
                yk_ref[pl.ds(base * 16 + a * 4 + k, 8, stride=16), :] = wy * carried[k]
            wz_ref[pl.ds(base * 8 + a, 8, stride=8), :] = spline(oz + (0.5 - a))
            wz_ref[pl.ds(base * 8 + 4 + a, 8, stride=8), :] = zero8

    def prepare(i, carry):
        base = pl.multiple_of(i * 8, 8)
        live = jnp.zeros((8, LANES), jnp.int32)
        for s in range(8):
            count = jnp.where(owner_ref[base + s] == myself, count_ref[base + s], 0)
            live = jnp.where(sub == s, count, live)
        at = pl.ds(base, 8)
        mass = jnp.where(lane < live, mass_ref[at, :], 0.0)
        carried = [mass] + [mass * vel_ref[j, at, :] for j in range(3)]
        fill(base, offs_ref[0, at, :], offs_ref[1, at, :], offs_ref[2, at, :], carried)
        return carry

    lax.fori_loop(0, rows // 8, prepare, 0)
    for group in range(came // 64):
        part = [box_ref[pl.ds(group * 64 + c, 8, stride=8), :] for c in range(8)]
        carried = [part[3]] + [part[3] * part[4 + j] for j in range(3)]
        fill(rows + group * 8, part[0], part[1], part[2], carried)
    for group in range(rows + came // 8, total, 8):
        fill(group, zero8, zero8, zero8, [zero8] * 4)
    for row in range(rows, total):
        block_ref[row] = came_ref[row - rows] if row < rows + came // 8 else 0

    def stencil(row):
        parts = []
        yk = yk_ref[pl.ds(pl.multiple_of(row * 16, 16), 16), :]
        for a in range(4):
            parts.append(yk * wx_ref[pl.ds(row * 4 + a, 1), :])
        left = jnp.concatenate(parts, 0)
        high = left.astype(jnp.bfloat16)
        low = (left - high.astype(jnp.float32)).astype(jnp.bfloat16)
        wz = wz_ref[pl.ds(pl.multiple_of(row * 8, 8), 8), :]
        zhigh = wz.astype(jnp.bfloat16)
        zlow = (wz - zhigh.astype(jnp.float32)).astype(jnp.bfloat16)
        lhs = jnp.concatenate([high, low, high], 1)
        rhs = jnp.concatenate([zhigh, zhigh, zlow], 1)
        rhs = jnp.concatenate([rhs, jnp.zeros((LANES - 8, 3 * LANES), jnp.bfloat16)], 0)
        return lax.dot_general(lhs, rhs, (((1,), (1,)), ((), ())), preferred_element_type=jnp.float32)

    def place(block, sums):
        base_x = 2 * lax.div(block, half_y * half_z)
        rest = lax.rem(block, half_y * half_z)
        base_y = lax.div(rest, half_z)
        base_z = lax.rem(rest, half_z)
        layer = jnp.where(base_z == 0, planes, jnp.where(base_z == half_z - 1, 2 * planes, 0))
        shift = lax.rem(2 * base_z + LANES - 1, LANES)
        sums = pltpu.roll(sums, shift, 1)
        at = pl.ds(pl.multiple_of(base_y * 8, 8), 16)
        for a in range(4):
            spot = layer + base_x + a
            grid_ref[spot, at, :] = grid_ref[spot, at, :] + sums[a * 16 : a * 16 + 16]

    half = row_half
    even_ref[...] = jnp.zeros(even_ref.shape, jnp.float32)
    odd_ref[...] = jnp.zeros(odd_ref.shape, jnp.float32)

    def row_group(i, carry):
        base = i * 2 * half
        for s in range(half):
            even_ref[s] = stencil(base + s)
        for s in range(half):
            place(block_ref[jnp.maximum(base - half + s, 0)], odd_ref[s])
        for s in range(half):
            odd_ref[s] = stencil(base + half + s)
        for s in range(half):
            place(block_ref[base + s], even_ref[s])
        return carry

    lax.fori_loop(0, total // (2 * half), row_group, 0)
    for s in range(half):
        place(block_ref[total - half + s], odd_ref[s])

    def finish(i, carry):
        at = pl.ds(pl.multiple_of(i * 8, 8), 8)
        low, high = zero8, zero8
        for x in range(planes):
            first = grid_ref[planes + x, at, :]
            last = grid_ref[2 * planes + x, at, :]
            main = grid_ref[x, at, :] + jnp.where(lane < LANES - 1, first, 0.0) + jnp.where(lane > 0, last, 0.0)
            out_ref[x, at, :] = main
            low = jnp.where(lane == x, pltpu.roll(first, x + 1, 1), low)
            low = jnp.where(lane == 16 + x, pltpu.roll(main, 16 + x, 1), low)
            high = jnp.where(lane == x, pltpu.roll(last, x, 1) if x else last, high)
            high = jnp.where(lane == 16 + x, pltpu.roll(main, 17 + x, 1), high)
        out_ref[planes, at, :] = low
        out_ref[planes + 1, at, :] = high
        return carry

    lax.fori_loop(0, out_ref.shape[1] // 8, finish, 0)


def halo_kernel(
    counts, grid_in, out_ref, z_box, y_box, x_box, c_box, edge_ref, e_out, e_box, col_ref, send_sem, recv_sem
):
    planes = out_ref.shape[0] - 2
    tall = out_ref.shape[1]
    chunks = tall // 8
    blocks = edge_ref.shape[0] // LANES
    sides = neighbours(counts)
    lane = lax.broadcasted_iota(jnp.int32, (8, LANES), 1)
    for box in (z_box, y_box, x_box, c_box, e_box):
        box[...] = jnp.zeros_like(box)
    greet(sides)()
    first, last = pl.ds(0, 8), pl.ds(tall - 8, 8)

    def begin(way, source, target_ref, sem):
        axis, target, there, other = sides[way]
        copy = remote(source, target_ref, send_sem.at[sem], recv_sem.at[sem], axis, target)
        pl.when(there)(copy.start)
        return copy, there, other

    def end(copies):
        for copy, there, other in copies:
            pl.when(there)(copy.wait_send)
            pl.when(other)(copy.wait_recv)

    def roll(value, shift):
        shift = shift % LANES
        return pltpu.roll(value, shift, 1) if shift else value

    bulk = [
        begin(0, grid_in.at[pl.ds(0, 2)], x_box.at[0], 0),
        begin(1, grid_in.at[pl.ds(planes - 2, 2)], x_box.at[1], 1),
    ]
    end([
        begin(4, grid_in.at[planes], z_box.at[0], 4),
        begin(5, grid_in.at[planes + 1], z_box.at[1], 5),
    ])

    def add_z(i, carry):
        at = pl.ds(i * 8 if isinstance(i, int) else pl.multiple_of(i * 8, 8), 8)
        above, below = z_box[0, at, :], z_box[1, at, :]
        for x in range(planes):
            main = grid_in[x, at, :]
            main = main + jnp.where(lane == LANES - 1, roll(above, LANES - 1 - x), 0.0)
            out_ref[x, at, :] = main + jnp.where(lane == 0, roll(below, -x), 0.0)
        out_ref[planes, at, :] = grid_in[planes, at, :] + roll(below, -16)
        out_ref[planes + 1, at, :] = grid_in[planes + 1, at, :] + roll(above, -16)
        return carry

    add_z(0, 0)
    add_z(chunks - 1, 0)
    across = [
        begin(2, out_ref.at[:, first, :], y_box.at[0], 2),
        begin(3, out_ref.at[:, last, :], y_box.at[1], 3),
    ]
    lax.fori_loop(1, chunks - 1, add_z, 0)
    end(across)
    corner = [
        begin(0, y_box.at[:, pl.ds(0, 2)], c_box.at[0], 6),
        begin(1, y_box.at[:, pl.ds(planes - 2, 2)], c_box.at[1], 7),
    ]
    for x in range(planes + 2):
        out_ref[x, last, :] = out_ref[x, last, :] + y_box[0, x]
        out_ref[x, first, :] = out_ref[x, first, :] + y_box[1, x]

    def pack(i, carry):
        at = pl.ds(pl.multiple_of(i * 8, 8), 8)
        zlow, zhigh = out_ref[planes, at, :], out_ref[planes + 1, at, :]
        above, below = z_box[0, at, :], z_box[1, at, :]
        value = jnp.where(lane == 0, zlow, jnp.where(lane == 1, roll(zhigh, 1), 0.0))
        value = jnp.where(lane == 8, roll(zlow, 8 - (planes - 1)), value)
        value = jnp.where(lane == 9, roll(zhigh, 9 - (planes - 1)), value)
        value = jnp.where((lane == 2) | (lane == 3), roll(above, 2), value)
        value = jnp.where((lane == 4) | (lane == 5), roll(below, 4), value)
        value = jnp.where((lane == 10) | (lane == 11), roll(above, 10 - (planes - 2)), value)
        value = jnp.where((lane == 12) | (lane == 13), roll(below, 12 - (planes - 2)), value)
        edge_ref[at, :] = value
        return carry

    lax.fori_loop(0, chunks, pack, 0)
    edge_ref[pl.ds(tall, blocks * LANES - tall), :] = jnp.zeros((blocks * LANES - tall, LANES), jnp.float32)
    for block in range(blocks):
        at = pl.ds(block * LANES, LANES)
        turned = jnp.transpose(edge_ref[at, :])
        e_out[0, :, at] = turned[0:8]
        e_out[1, :, at] = turned[8:16]
    corner = corner + [begin(0, e_out.at[0], e_box.at[0], 8), begin(1, e_out.at[1], e_box.at[1], 9)]
    end(bulk)
    end(corner)
    for block in range(blocks):
        at = pl.ds(block * LANES, LANES)
        both = jnp.concatenate(
            [e_box[0, :, at], e_box[1, :, at], jnp.zeros((LANES - 16, LANES), jnp.float32)], 0
        )
        col_ref[at, :] = jnp.transpose(both)
    for p in range(2):
        high, low = planes - 2 + p, p
        out_ref[high, last, :] = out_ref[high, last, :] + c_box[0, 0, p]
        out_ref[high, first, :] = out_ref[high, first, :] + c_box[0, 1, p]
        out_ref[low, last, :] = out_ref[low, last, :] + c_box[1, 0, p]
        out_ref[low, first, :] = out_ref[low, first, :] + c_box[1, 1, p]

    def add_x(i, carry):
        at = pl.ds(pl.multiple_of(i * 8, 8), 8)
        col = col_ref[at, :]

        def put(spot, source):
            return jnp.where(lane == spot, roll(col, spot - source), 0.0)

        for p in range(2):
            high, low = planes - 2 + p, p
            out_ref[high, at, :] = (
                out_ref[high, at, :] + x_box[0, p, at, :] + put(LANES - 1, 2 + p) + put(0, 4 + p)
            )
            out_ref[low, at, :] = (
                out_ref[low, at, :] + x_box[1, p, at, :] + put(LANES - 1, 10 + p) + put(0, 12 + p)
            )
        for side in range(2):
            out_ref[planes + side, at, :] = (
                out_ref[planes + side, at, :] + put(planes - 2, side) + put(1, 8 + side)
            )
        return carry

    lax.fori_loop(0, chunks, add_x, 0)


def update_kernel(counts, grid_ref, mat_ref, stiff_ref, mass_ref, vel_ref, v_ref, z_ref):
    span_x, span_y, span_z = mass_ref.shape
    planes = span_x + 2
    there = [side[2].astype(jnp.float32) for side in neighbours(counts)]
    lane = lax.broadcasted_iota(jnp.int32, (span_y, LANES), 1)
    bottom = jnp.logical_and(lane == 0, jnp.logical_not(lax.axis_index("gz") > 0))

    def speeds(x, start, length, scale):
        def read(k):
            if length == 1:
                return grid_ref[x, pl.ds(start * 4 + k, 1), :]
            return grid_ref[x, pl.ds(start * 4 + k, length, stride=4), :]

        under = scale / jnp.maximum(read(0), 1.0)
        return [read(1 + j) * under for j in range(3)]

    def fill(x, carry):
        scale = jnp.where(x == 0, there[0], jnp.where(x == planes - 1, there[1], 1.0))
        for j, value in enumerate(speeds(x, 1, span_y, scale)):
            v_ref[j, x, pl.ds(8, span_y), :] = value
        for j, value in enumerate(speeds(x, 0, 1, there[2])):
            v_ref[j, x, pl.ds(7, 1), :] = value
        for j, value in enumerate(speeds(x, span_y + 1, 1, there[3])):
            v_ref[j, x, pl.ds(8 + span_y, 1), :] = value
        return carry

    lax.fori_loop(0, planes, fill, 0)
    for side in range(2):
        for j, value in enumerate(speeds(planes + side, 1, span_y, there[4 + side])):
            z_ref[side, j] = value

    def update(x, carry):
        mass_ref[x] = grid_ref[x + 1, pl.ds(4, span_y, stride=4), :]
        material = mat_ref[x]
        stiff = jnp.zeros((span_y, LANES), jnp.float32)
        for m in range(stiff_ref.shape[0]):
            stiff = jnp.where(material == m, stiff_ref[m], stiff)
        for j in range(3):
            value = v_ref[j, x + 1, pl.ds(8, span_y), :]
            beside = v_ref[j, x + 2, pl.ds(8, span_y), :] + v_ref[j, x, pl.ds(8, span_y), :]
            beside = beside + v_ref[j, x + 1, pl.ds(9, span_y), :] + v_ref[j, x + 1, pl.ds(7, span_y), :]
            after = pltpu.roll(z_ref[1, j], LANES - 2 - x, 1)
            before = pltpu.roll(z_ref[0, j], LANES - 1 - x, 1)
            beside = beside + jnp.where(lane == LANES - 1, after, pltpu.roll(value, LANES - 1, 1))
            beside = beside + jnp.where(lane == 0, before, pltpu.roll(value, 1, 1))
            result = value + stiff * (beside - 6.0 * value)
            if j == 2:
                result = result - gravity_step
                result = jnp.where(bottom, jnp.maximum(result, 0.0), result)
            vel_ref[j, x] = result
        return carry

    lax.fori_loop(0, span_x, update, 0)


def per_device(
    counts, row_owner, row_count, row_block, offsets, particle_mass, particle_velocity, material, stiffness
):
    rows = particle_mass.shape[0]
    span_x, span_y, span_z = material.shape
    planes = span_x + 2
    tall = (span_y + 2) * 4
    wide = pl.cdiv(tall, LANES) * LANES
    f32 = jnp.float32
    vmem = pl.BlockSpec(memory_space=pltpu.VMEM)
    hbm = pl.BlockSpec(memory_space=pl.ANY)
    smem = pl.BlockSpec(memory_space=pltpu.SMEM)
    myself = (lax.axis_index("gx") * counts["gy"] + lax.axis_index("gy")) * counts["gz"] + lax.axis_index("gz")

    box = pl.pallas_call(
        functools.partial(rows_kernel, counts),
        out_shape=jax.ShapeDtypeStruct((6, CAP, 8, LANES), f32),
        in_specs=[hbm] * 6,
        out_specs=vmem,
        scratch_shapes=[
            pltpu.VMEM((rows // LANES, LANES), jnp.int32),
            pltpu.SMEM((rows,), jnp.int32),
            pltpu.SMEM((rows,), jnp.int32),
            pltpu.VMEM(offsets.shape, f32),
            pltpu.VMEM(particle_mass.shape, f32),
            pltpu.VMEM(particle_velocity.shape, f32),
            pltpu.VMEM((6, CAP, 8, LANES), f32),
            pltpu.SemaphoreType.DMA((6,)),
            pltpu.SemaphoreType.DMA((6,)),
            pltpu.SemaphoreType.DMA((6,)),
        ],
        compiler_params=pltpu.CompilerParams(
            collective_id=0, has_side_effects=True, vmem_limit_bytes=VMEM_WHOLE
        ),
        name="row_exchange",
    )(row_owner.reshape(-1, LANES), row_count, row_block, offsets, particle_mass, particle_velocity)

    came_blocks = box[:, :, 7, 0].reshape(-1).astype(jnp.int32)
    half = 16
    total = pl.cdiv(rows + 6 * CAP, 2 * half) * 2 * half
    grid = pl.pallas_call(
        functools.partial(deposit_kernel, span_y // 2, span_z // 2, planes),
        out_shape=jax.ShapeDtypeStruct((planes + 2, tall, LANES), f32),
        in_specs=[smem] * 2 + [hbm] * 6 + [vmem],
        out_specs=vmem,
        scratch_shapes=[
            pltpu.SMEM((rows,), jnp.int32),
            pltpu.SMEM((rows,), jnp.int32),
            pltpu.SMEM((total,), jnp.int32),
            pltpu.VMEM(offsets.shape, f32),
            pltpu.VMEM(particle_mass.shape, f32),
            pltpu.VMEM(particle_velocity.shape, f32),
            pltpu.SemaphoreType.DMA((6,)),
            pltpu.VMEM((3 * planes, tall, LANES), f32),
            pltpu.VMEM((total * 4, LANES), f32),
            pltpu.VMEM((total * 16, LANES), f32),
            pltpu.VMEM((total * 8, LANES), f32),
            pltpu.VMEM((half, 64, LANES), f32),
            pltpu.VMEM((half, 64, LANES), f32),
        ],
        compiler_params=pltpu.CompilerParams(vmem_limit_bytes=VMEM_LIMIT),
        name="deposit",
    )(
        myself.reshape(1), came_blocks, row_owner, row_count, row_block,
        offsets, particle_mass, particle_velocity, box.reshape(6 * CAP * 8, LANES),
    )

    grid = pl.pallas_call(
        functools.partial(halo_kernel, counts),
        out_shape=jax.ShapeDtypeStruct((planes + 2, tall, LANES), f32),
        in_specs=[vmem],
        out_specs=vmem,
        scratch_shapes=[
            pltpu.VMEM((2, tall, LANES), f32),
            pltpu.VMEM((2, planes + 2, 8, LANES), f32),
            pltpu.VMEM((2, 2, tall, LANES), f32),
            pltpu.VMEM((2, 2, 2, 8, LANES), f32),
            pltpu.VMEM((wide, LANES), f32),
            pltpu.VMEM((2, 8, wide), f32),
            pltpu.VMEM((2, 8, wide), f32),
            pltpu.VMEM((wide, LANES), f32),
            pltpu.SemaphoreType.DMA((10,)),
            pltpu.SemaphoreType.DMA((10,)),
        ],
        compiler_params=pltpu.CompilerParams(
            collective_id=1, has_side_effects=True, vmem_limit_bytes=VMEM_LIMIT
        ),
        name="halo_sums",
    )(grid)

    return pl.pallas_call(
        functools.partial(update_kernel, counts),
        out_shape=(
            jax.ShapeDtypeStruct((span_x, span_y, span_z), f32),
            jax.ShapeDtypeStruct((3, span_x, span_y, span_z), f32),
        ),
        in_specs=[vmem, vmem, smem],
        out_specs=(vmem, vmem),
        scratch_shapes=[
            pltpu.VMEM((3, planes, span_y + 16, LANES), f32),
            pltpu.VMEM((2, 3, span_y, LANES), f32),
        ],
        compiler_params=pltpu.CompilerParams(vmem_limit_bytes=VMEM_LIMIT),
        name="grid_update",
    )(grid, material, stiffness)


def solution(mesh):
    placed = (
        P(("runs", "gx", "gy", "gz")),
        P(("runs", "gx", "gy", "gz")),
        P(("runs", "gx", "gy", "gz")),
        P(None, ("runs", "gx", "gy", "gz"), None),
        P(("runs", "gx", "gy", "gz"), None),
        P(None, ("runs", "gx", "gy", "gz"), None),
        P(("runs", "gx"), "gy", "gz"),
        P(),
    )
    counts = {axis: mesh.shape[axis] for axis in AXES}
    return jax.shard_map(
        functools.partial(per_device, counts),
        mesh=mesh,
        in_specs=placed,
        out_specs=(P(("runs", "gx"), "gy", "gz"), P(None, ("runs", "gx"), "gy", "gz")),
        check_vma=False,
    )
```

```python
import functools

import jax
import jax.numpy as jnp
from jax import lax
from jax.experimental import pallas as pl
from jax.experimental.pallas import tpu as pltpu
from jax.sharding import PartitionSpec as P

CAP = 4
LANES = 128
gravity_step = 0.05
AXES = ("gx", "gy", "gz")
VMEM_LIMIT = 48 * 1024 * 1024
VMEM_WHOLE = 60 * 1024 * 1024


def spline(distance):
    distance = jnp.abs(distance)
    inside_part = 0.75 - distance * distance
    rest = jnp.maximum(1.5 - distance, 0.0)
    return jnp.where(distance < 0.5, inside_part, 0.5 * rest * rest)


def neighbours(counts):
    found = []
    for axis in AXES:
        here = lax.axis_index(axis)
        low = here > 0
        high = here < counts[axis] - 1
        found.append((axis, here - 1, low, high))
        found.append((axis, here + 1, high, low))
    return found


def greet(sides):
    barrier = pltpu.get_barrier_semaphore()
    total = 0
    for axis, target, there, _ in sides:
        @pl.when(there)
        def _():
            pl.semaphore_signal(
                barrier, inc=1, device_id={axis: target}, device_id_type=pl.DeviceIdType.MESH
            )
        total = total + there.astype(jnp.int32)
    return lambda: pl.semaphore_wait(barrier, total)


def load(sources, targets, sems):
    copies = [pltpu.make_async_copy(s, t, sems.at[n]) for n, (s, t) in enumerate(zip(sources, targets))]
    for copy in copies:
        copy.start()
    return copies


def remote(source, target_ref, send_sem, recv_sem, axis, target):
    return pltpu.make_async_remote_copy(
        src_ref=source,
        dst_ref=target_ref,
        send_sem=send_sem,
        recv_sem=recv_sem,
        device_id={axis: target},
        device_id_type=pl.DeviceIdType.MESH,
    )


def rows_kernel(
    counts, owner_in, count_in, block_in, offs_in, mass_in, vel_in, box_ref, head_ref,
    owner_ref, count_ref, block_ref, offs_ref, mass_ref, vel_ref, out_box, load_sem, send_sem, recv_sem,
):
    loads = load(
        (owner_in, count_in, block_in, offs_in, mass_in, vel_in),
        (owner_ref, count_ref, block_ref, offs_ref, mass_ref, vel_ref),
        load_sem,
    )
    rows = mass_ref.shape[0]
    size_y, size_z = counts["gy"], counts["gz"]
    myself = (lax.axis_index("gx") * size_y + lax.axis_index("gy")) * size_z + lax.axis_index("gz")
    sides = neighbours(counts)
    box_ref[...] = jnp.zeros_like(box_ref)
    greeted = greet(sides)
    loads[0].wait()
    heading = owner_ref[...] - myself
    shape = heading.shape
    place = lax.broadcasted_iota(jnp.int32, shape, 0) * LANES + lax.broadcasted_iota(jnp.int32, shape, 1)
    lane = lax.broadcasted_iota(jnp.int32, (1, LANES), 1)
    steps = (-size_y * size_z, size_y * size_z, -size_z, size_z, -1, 1)
    left = [jnp.where(heading == step, place, rows) for step in steps]
    for copy in loads[1:]:
        copy.wait()
    for slot in range(CAP):
        for way in range(6):
            first = jnp.min(left[way])
            left[way] = jnp.where(left[way] == first, rows, left[way])
            valid = first < rows
            row = jnp.minimum(first, rows - 1)
            live = jnp.where(valid, count_ref[row], 0)
            for j in range(3):
                out_box[way, slot, pl.ds(j, 1), :] = offs_ref[j, pl.ds(row, 1), :]
                out_box[way, slot, pl.ds(4 + j, 1), :] = vel_ref[j, pl.ds(row, 1), :]
            out_box[way, slot, pl.ds(3, 1), :] = jnp.where(lane < live, mass_ref[pl.ds(row, 1), :], 0.0)
            block = jnp.where(valid, block_ref[row], 0).astype(jnp.float32)
            out_box[way, slot, pl.ds(7, 1), :] = jnp.full((1, LANES), block, jnp.float32)
    greeted()
    copies = [
        remote(out_box.at[way], box_ref.at[way], send_sem.at[way], recv_sem.at[way], axis, target)
        for way, (axis, target, _, _) in enumerate(sides)
    ]
    for way, (_, _, there, _) in enumerate(sides):
        pl.when(there)(copies[way].start)
    for way, (_, _, there, other) in enumerate(sides):
        pl.when(there)(copies[way].wait_send)
        pl.when(other)(copies[way].wait_recv)
    for way in range(6):
        for slot in range(CAP):
            head_ref[pl.ds(way * CAP + slot, 1), :] = box_ref[way, slot, pl.ds(7, 1), :]


def deposit_kernel(
    half_y, half_z, planes, me_ref, came_in, owner_in, count_in, block_in, offs_in, mass_in, vel_in,
    box_ref, out_ref, owner_ref, count_ref, block_ref, offs_ref, mass_ref, vel_ref, came_ref, load_sem,
    grid_ref, wx_ref, yk_ref, wz_ref, even_ref, odd_ref,
):
    loads = load(
        (owner_in, count_in, block_in, offs_in, mass_in, vel_in, came_in),
        (owner_ref, count_ref, block_ref.at[pl.ds(0, mass_ref.shape[0])], offs_ref, mass_ref, vel_ref, came_ref),
        load_sem,
    )
    rows = mass_ref.shape[0]
    came = box_ref.shape[0]
    total = block_ref.shape[0]
    row_half = even_ref.shape[0]
    sub = lax.broadcasted_iota(jnp.int32, (8, LANES), 0)
    lane = lax.broadcasted_iota(jnp.int32, (8, LANES), 1)
    myself = me_ref[0]
    zero8 = jnp.zeros((8, LANES), jnp.float32)
    low_pair = lax.shift_right_logical((lane + LANES - 1) & (LANES - 1), 1)
    high_pair = lax.shift_right_logical((lane + 1) & (LANES - 1), 1)

    def clear(i, carry):
        grid_ref[i] = jnp.zeros(grid_ref.shape[1:], jnp.float32)
        return carry

    lax.fori_loop(0, grid_ref.shape[0], clear, 0)
    for copy in loads:
        copy.wait()

    def fill(base, ox, oy, oz, carried):
        for a in range(4):
            wx_ref[pl.ds(base * 4 + a, 8, stride=4), :] = spline(ox + (0.5 - a))
            wy = spline(oy + (0.5 - a))
            for k in range(4):
                yk_ref[pl.ds(base * 16 + a * 4 + k, 8, stride=16), :] = wy * carried[k]
            wz_ref[pl.ds(base * 8 + a, 8, stride=8), :] = spline(oz + (0.5 - a))
            wz_ref[pl.ds(base * 8 + 4 + a, 8, stride=8), :] = zero8

    def prepare(i, carry):
        base = pl.multiple_of(i * 8, 8)
        live = jnp.zeros((8, LANES), jnp.int32)
        for s in range(8):
            count = jnp.where(owner_ref[base + s] == myself, count_ref[base + s], 0)
            live = jnp.where(sub == s, count, live)
        at = pl.ds(base, 8)
        mass = jnp.where(lane < live, mass_ref[at, :], 0.0)
        carried = [mass] + [mass * vel_ref[j, at, :] for j in range(3)]
        fill(base, offs_ref[0, at, :], offs_ref[1, at, :], offs_ref[2, at, :], carried)
        return carry

    lax.fori_loop(0, rows // 8, prepare, 0)
    for group in range(came // 64):
        part = [box_ref[pl.ds(group * 64 + c, 8, stride=8), :] for c in range(8)]
        carried = [part[3]] + [part[3] * part[4 + j] for j in range(3)]
        fill(rows + group * 8, part[0], part[1], part[2], carried)
    for group in range(rows + came // 8, total, 8):
        fill(group, zero8, zero8, zero8, [zero8] * 4)
    for row in range(rows, total):
        block_ref[row] = came_ref[row - rows, 0].astype(jnp.int32) if row < rows + came // 8 else 0

    def stencil(row):
        parts = []
        yk = yk_ref[pl.ds(pl.multiple_of(row * 16, 16), 16), :]
        for a in range(4):
            parts.append(yk * wx_ref[pl.ds(row * 4 + a, 1), :])
        left = jnp.concatenate(parts, 0)
        high = left.astype(jnp.bfloat16)
        low = (left - high.astype(jnp.float32)).astype(jnp.bfloat16)
        wz = wz_ref[pl.ds(pl.multiple_of(row * 8, 8), 8), :]
        zhigh = wz.astype(jnp.bfloat16)
        zlow = (wz - zhigh.astype(jnp.float32)).astype(jnp.bfloat16)
        lhs = jnp.concatenate([high, low, high], 1)
        rhs = jnp.concatenate([zhigh, zhigh, zlow], 1)
        rhs = jnp.concatenate([rhs, jnp.zeros((LANES - 8, 3 * LANES), jnp.bfloat16)], 0)
        return lax.dot_general(lhs, rhs, (((1,), (1,)), ((), ())), preferred_element_type=jnp.float32)

    def place(block, sums):
        base_x = 2 * lax.div(block, half_y * half_z)
        rest = lax.rem(block, half_y * half_z)
        base_y = lax.div(rest, half_z)
        base_z = lax.rem(rest, half_z)
        layer = jnp.where(base_z == 0, planes, jnp.where(base_z == half_z - 1, 2 * planes, 0))
        shift = lax.rem(2 * base_z + LANES - 1, LANES)
        sums = pltpu.roll(sums, shift, 1)
        at = pl.ds(pl.multiple_of(base_y * 8, 8), 16)
        for a in range(4):
            spot = layer + base_x + a
            grid_ref[spot, at, :] = grid_ref[spot, at, :] + sums[a * 16 : a * 16 + 16]

    half = row_half
    even_ref[...] = jnp.zeros(even_ref.shape, jnp.float32)
    odd_ref[...] = jnp.zeros(odd_ref.shape, jnp.float32)

    def row_group(i, carry):
        base = i * 2 * half
        for s in range(half):
            even_ref[s] = stencil(base + s)
        for s in range(half):
            place(block_ref[jnp.maximum(base - half + s, 0)], odd_ref[s])
        for s in range(half):
            odd_ref[s] = stencil(base + half + s)
        for s in range(half):
            place(block_ref[base + s], even_ref[s])
        return carry

    lax.fori_loop(0, total // (2 * half), row_group, 0)
    for s in range(half):
        place(block_ref[total - half + s], odd_ref[s])

    def finish(i, carry):
        at = pl.ds(pl.multiple_of(i * 8, 8), 8)
        low, high = zero8, zero8
        for x in range(planes):
            first = grid_ref[planes + x, at, :]
            last = grid_ref[2 * planes + x, at, :]
            main = grid_ref[x, at, :] + jnp.where(lane < LANES - 1, first, 0.0) + jnp.where(lane > 0, last, 0.0)
            out_ref[x, at, :] = main
            below = pltpu.roll(jnp.where(lane == LANES - 1, first, main), 2 * x + 2, 1)
            above = jnp.where(lane == 0, last, main)
            above = pltpu.roll(above, 2 * x, 1) if x else above
            low = jnp.where(low_pair == x, below, low)
            high = jnp.where(high_pair == x, above, high)
        out_ref[planes, at, :] = low
        out_ref[planes + 1, at, :] = high
        return carry

    lax.fori_loop(0, out_ref.shape[1] // 8, finish, 0)


def halo_kernel(
    counts, grid_in, out_ref, z_box, y_box, x_box, c_box, edge_ref, e_out, e_box, col_ref, send_sem, recv_sem
):
    planes = out_ref.shape[0] - 1
    tall = out_ref.shape[1]
    chunks = tall // (24 if tall % 24 == 0 else 8)
    blocks = edge_ref.shape[0] // LANES
    sides = neighbours(counts)
    tile = 24 if tall % 24 == 0 else 8
    lane = lax.broadcasted_iota(jnp.int32, (tile, LANES), 1)
    odd = (lane & 1) == 1
    rim = jnp.logical_or(lane == 0, lane == LANES - 1)
    for box in (z_box, y_box, x_box, c_box, e_box):
        box[...] = jnp.zeros_like(box)
    greet(sides)()
    first, last = pl.ds(0, 8), pl.ds(tall - 8, 8)

    def begin(way, source, target_ref, sem):
        axis, target, there, other = sides[way]
        copy = remote(source, target_ref, send_sem.at[sem], recv_sem.at[sem], axis, target)
        pl.when(there)(copy.start)
        return copy, there, other

    def end(copies):
        for copy, there, other in copies:
            pl.when(there)(copy.wait_send)
            pl.when(other)(copy.wait_recv)

    def roll(value, shift):
        shift = shift % LANES
        return pltpu.roll(value, shift, 1) if shift else value

    bulk = [
        begin(0, grid_in.at[pl.ds(0, 2)], x_box.at[0], 0),
        begin(1, grid_in.at[pl.ds(planes - 2, 2)], x_box.at[1], 1),
    ]
    end([
        begin(4, grid_in.at[planes], z_box.at[0], 4),
        begin(5, grid_in.at[planes + 1], z_box.at[1], 5),
    ])

    def received(at):
        return jnp.where(odd, z_box[0, at, :], roll(z_box[1, at, :], 2))

    def add_z(i, carry):
        at = pl.ds(i * tile if isinstance(i, int) else pl.multiple_of(i * tile, 8), tile)
        both = received(at)
        for x in range(planes):
            out_ref[x, at, :] = grid_in[x, at, :] + jnp.where(rim, roll(both, LANES - 2 - 2 * x), 0.0)
        low = grid_in[planes, at, :] + roll(z_box[1, at, :], 2)
        high = grid_in[planes + 1, at, :] + roll(z_box[0, at, :], -2)
        out_ref[planes, at, :] = jnp.where(odd, low, high)
        return carry

    add_z(0, 0)
    add_z(chunks - 1, 0)
    across = [
        begin(2, out_ref.at[:, first, :], y_box.at[0], 2),
        begin(3, out_ref.at[:, last, :], y_box.at[1], 3),
    ]
    lax.fori_loop(1, chunks - 1, add_z, 0)
    end(across)
    corner = [
        begin(0, y_box.at[:, pl.ds(0, 2)], c_box.at[0], 6),
        begin(1, y_box.at[:, pl.ds(planes - 2, 2)], c_box.at[1], 7),
    ]
    for x in range(planes + 1):
        out_ref[x, last, :] = out_ref[x, last, :] + y_box[0, x]
        out_ref[x, first, :] = out_ref[x, first, :] + y_box[1, x]

    def pack(i, carry):
        at = pl.ds(pl.multiple_of(i * tile, 8), tile)
        zone = out_ref[planes, at, :]
        both = received(at)
        value = jnp.where(lane < 14, roll(both, 10 - (2 * planes - 3)), 0.0)
        value = jnp.where(lane < 10, roll(zone, 8 - (2 * planes - 2)), value)
        value = jnp.where(lane < 8, 0.0, value)
        value = jnp.where(lane < 6, roll(both, 1), value)
        value = jnp.where(lane < 2, zone, value)
        edge_ref[at, :] = value
        return carry

    lax.fori_loop(0, chunks, pack, 0)
    edge_ref[pl.ds(tall, blocks * LANES - tall), :] = jnp.zeros((blocks * LANES - tall, LANES), jnp.float32)
    for block in range(blocks):
        at = pl.ds(block * LANES, LANES)
        turned = jnp.transpose(edge_ref[at, :])
        e_out[0, :, at] = turned[0:8]
        e_out[1, :, at] = turned[8:16]
    corner = corner + [begin(0, e_out.at[0], e_box.at[0], 8), begin(1, e_out.at[1], e_box.at[1], 9)]
    end(bulk)
    end(corner)
    for block in range(blocks):
        at = pl.ds(block * LANES, LANES)
        both = jnp.concatenate(
            [e_box[0, :, at], e_box[1, :, at], jnp.zeros((LANES - 16, LANES), jnp.float32)], 0
        )
        col_ref[at, :] = jnp.transpose(both)
    for p in range(2):
        high, low = planes - 2 + p, p
        out_ref[high, last, :] = out_ref[high, last, :] + c_box[0, 0, p]
        out_ref[high, first, :] = out_ref[high, first, :] + c_box[0, 1, p]
        out_ref[low, last, :] = out_ref[low, last, :] + c_box[1, 0, p]
        out_ref[low, first, :] = out_ref[low, first, :] + c_box[1, 1, p]

    def add_x(i, carry):
        at = pl.ds(pl.multiple_of(i * tile, 8), tile)
        col = col_ref[at, :]

        def put(source):
            return jnp.where(rim, roll(col, LANES - 1 - source), 0.0)

        for p in range(2):
            high, low = planes - 2 + p, p
            out_ref[high, at, :] = out_ref[high, at, :] + x_box[0, p, at, :] + put(2 + 2 * p)
            out_ref[low, at, :] = out_ref[low, at, :] + x_box[1, p, at, :] + put(10 + 2 * p)
        last_pair = jnp.where((lane == 2 * planes - 4) | (lane == 2 * planes - 3), roll(col, 2 * planes - 4), 0.0)
        first_pair = jnp.where((lane == 2) | (lane == 3), roll(col, -6), 0.0)
        out_ref[planes, at, :] = out_ref[planes, at, :] + last_pair + first_pair
        return carry

    lax.fori_loop(0, chunks, add_x, 0)


def update_kernel(counts, grid_ref, mat_ref, stiff_ref, mass_ref, vel_ref, v_ref, z_ref):
    span_x, span_y, span_z = mass_ref.shape
    planes = span_x + 2
    there = [side[2].astype(jnp.float32) for side in neighbours(counts)]
    lane = lax.broadcasted_iota(jnp.int32, (span_y, LANES), 1)
    bottom = jnp.logical_and(lane == 0, jnp.logical_not(lax.axis_index("gz") > 0))

    def speeds(x, start, length, scale):
        def read(k):
            if length == 1:
                return grid_ref[x, pl.ds(start * 4 + k, 1), :]
            return grid_ref[x, pl.ds(start * 4 + k, length, stride=4), :]

        under = scale / jnp.maximum(read(0), 1.0)
        return [read(1 + j) * under for j in range(3)]

    def fill(x, carry):
        scale = jnp.where(x == 0, there[0], jnp.where(x == planes - 1, there[1], 1.0))
        for j, value in enumerate(speeds(x, 1, span_y, scale)):
            v_ref[j, x, pl.ds(8, span_y), :] = value
        for j, value in enumerate(speeds(x, 0, 1, there[2])):
            v_ref[j, x, pl.ds(7, 1), :] = value
        for j, value in enumerate(speeds(x, span_y + 1, 1, there[3])):
            v_ref[j, x, pl.ds(8 + span_y, 1), :] = value
        return carry

    lax.fori_loop(0, planes, fill, 0)
    scale = jnp.where((lane & 1) == 1, there[4], there[5])
    for j, value in enumerate(speeds(planes, 1, span_y, scale)):
        z_ref[j] = value

    def update(x, carry):
        mass_ref[x] = grid_ref[x + 1, pl.ds(4, span_y, stride=4), :]
        material = mat_ref[x]
        stiff = jnp.zeros((span_y, LANES), jnp.float32)
        for m in range(stiff_ref.shape[0]):
            stiff = jnp.where(material == m, stiff_ref[m], stiff)
        for j in range(3):
            value = v_ref[j, x + 1, pl.ds(8, span_y), :]
            beside = v_ref[j, x + 2, pl.ds(8, span_y), :] + v_ref[j, x, pl.ds(8, span_y), :]
            beside = beside + v_ref[j, x + 1, pl.ds(9, span_y), :] + v_ref[j, x + 1, pl.ds(7, span_y), :]
            outside = pltpu.roll(z_ref[j], LANES - 3 - 2 * x, 1)
            beside = beside + jnp.where(lane == LANES - 1, outside, pltpu.roll(value, LANES - 1, 1))
            beside = beside + jnp.where(lane == 0, outside, pltpu.roll(value, 1, 1))
            result = value + stiff * (beside - 6.0 * value)
            if j == 2:
                result = result - gravity_step
                result = jnp.where(bottom, jnp.maximum(result, 0.0), result)
            vel_ref[j, x] = result
        return carry

    lax.fori_loop(0, span_x, update, 0)


def per_device(
    counts, row_owner, row_count, row_block, offsets, particle_mass, particle_velocity, material, stiffness
):
    rows = particle_mass.shape[0]
    span_x, span_y, span_z = material.shape
    planes = span_x + 2
    tall = (span_y + 2) * 4
    wide = pl.cdiv(tall, LANES) * LANES
    f32 = jnp.float32
    vmem = pl.BlockSpec(memory_space=pltpu.VMEM)
    hbm = pl.BlockSpec(memory_space=pl.ANY)
    smem = pl.BlockSpec(memory_space=pltpu.SMEM)
    myself = (lax.axis_index("gx") * counts["gy"] + lax.axis_index("gy")) * counts["gz"] + lax.axis_index("gz")

    box, heads = pl.pallas_call(
        functools.partial(rows_kernel, counts),
        out_shape=(
            jax.ShapeDtypeStruct((6, CAP, 8, LANES), f32),
            jax.ShapeDtypeStruct((6 * CAP, LANES), f32),
        ),
        in_specs=[hbm] * 6,
        out_specs=(vmem, vmem),
        scratch_shapes=[
            pltpu.VMEM((rows // LANES, LANES), jnp.int32),
            pltpu.SMEM((rows,), jnp.int32),
            pltpu.SMEM((rows,), jnp.int32),
            pltpu.VMEM(offsets.shape, f32),
            pltpu.VMEM(particle_mass.shape, f32),
            pltpu.VMEM(particle_velocity.shape, f32),
            pltpu.VMEM((6, CAP, 8, LANES), f32),
            pltpu.SemaphoreType.DMA((6,)),
            pltpu.SemaphoreType.DMA((6,)),
            pltpu.SemaphoreType.DMA((6,)),
        ],
        compiler_params=pltpu.CompilerParams(
            collective_id=0, has_side_effects=True, vmem_limit_bytes=VMEM_WHOLE
        ),
        name="row_exchange",
    )(row_owner.reshape(-1, LANES), row_count, row_block, offsets, particle_mass, particle_velocity)

    half = 16
    total = pl.cdiv(rows + 6 * CAP, 2 * half) * 2 * half
    grid = pl.pallas_call(
        functools.partial(deposit_kernel, span_y // 2, span_z // 2, planes),
        out_shape=jax.ShapeDtypeStruct((planes + 2, tall, LANES), f32),
        in_specs=[smem] + [hbm] * 7 + [vmem],
        out_specs=vmem,
        scratch_shapes=[
            pltpu.SMEM((rows,), jnp.int32),
            pltpu.SMEM((rows,), jnp.int32),
            pltpu.SMEM((total,), jnp.int32),
            pltpu.VMEM(offsets.shape, f32),
            pltpu.VMEM(particle_mass.shape, f32),
            pltpu.VMEM(particle_velocity.shape, f32),
            pltpu.SMEM((6 * CAP, LANES), f32),
            pltpu.SemaphoreType.DMA((7,)),
            pltpu.VMEM((3 * planes, tall, LANES), f32),
            pltpu.VMEM((total * 4, LANES), f32),
            pltpu.VMEM((total * 16, LANES), f32),
            pltpu.VMEM((total * 8, LANES), f32),
            pltpu.VMEM((half, 64, LANES), f32),
            pltpu.VMEM((half, 64, LANES), f32),
        ],
        compiler_params=pltpu.CompilerParams(vmem_limit_bytes=VMEM_LIMIT),
        name="deposit",
    )(
        myself.reshape(1), heads, row_owner, row_count, row_block,
        offsets, particle_mass, particle_velocity, box.reshape(6 * CAP * 8, LANES),
    )

    grid = pl.pallas_call(
        functools.partial(halo_kernel, counts),
        out_shape=jax.ShapeDtypeStruct((planes + 1, tall, LANES), f32),
        in_specs=[vmem],
        out_specs=vmem,
        scratch_shapes=[
            pltpu.VMEM((2, tall, LANES), f32),
            pltpu.VMEM((2, planes + 1, 8, LANES), f32),
            pltpu.VMEM((2, 2, tall, LANES), f32),
            pltpu.VMEM((2, 2, 2, 8, LANES), f32),
            pltpu.VMEM((wide, LANES), f32),
            pltpu.VMEM((2, 8, wide), f32),
            pltpu.VMEM((2, 8, wide), f32),
            pltpu.VMEM((wide, LANES), f32),
            pltpu.SemaphoreType.DMA((10,)),
            pltpu.SemaphoreType.DMA((10,)),
        ],
        compiler_params=pltpu.CompilerParams(
            collective_id=1, has_side_effects=True, vmem_limit_bytes=VMEM_LIMIT
        ),
        name="halo_sums",
    )(grid)

    return pl.pallas_call(
        functools.partial(update_kernel, counts),
        out_shape=(
            jax.ShapeDtypeStruct((span_x, span_y, span_z), f32),
            jax.ShapeDtypeStruct((3, span_x, span_y, span_z), f32),
        ),
        in_specs=[vmem, vmem, smem],
        out_specs=(vmem, vmem),
        scratch_shapes=[
            pltpu.VMEM((3, planes, span_y + 16, LANES), f32),
            pltpu.VMEM((3, span_y, LANES), f32),
        ],
        compiler_params=pltpu.CompilerParams(vmem_limit_bytes=VMEM_LIMIT),
        name="grid_update",
    )(grid, material, stiffness)


def solution(mesh):
    placed = (
        P(("runs", "gx", "gy", "gz")),
        P(("runs", "gx", "gy", "gz")),
        P(("runs", "gx", "gy", "gz")),
        P(None, ("runs", "gx", "gy", "gz"), None),
        P(("runs", "gx", "gy", "gz"), None),
        P(None, ("runs", "gx", "gy", "gz"), None),
        P(("runs", "gx"), "gy", "gz"),
        P(),
    )
    counts = {axis: mesh.shape[axis] for axis in AXES}
    return jax.shard_map(
        functools.partial(per_device, counts),
        mesh=mesh,
        in_specs=placed,
        out_specs=(P(("runs", "gx"), "gy", "gz"), P(None, ("runs", "gx"), "gy", "gz")),
        check_vma=False,
    )
```
